32 devices in a mesh: dp: 16 (over z, x, core), mp: 2 (over y).
Axes of the slice: x: 2, y: 2, z: 4, core: 2. Of those that a mesh axis runs over, the one named last changes fastest.
Arguments:
- session_length: int32 [16], P('dp'), may hold values from 1 to 128
- event_owner: int32 [2048, 1], P('dp'), may hold values from 0 to 15; in each aligned block of 128 rows (0 to 127, 128 to 255, ...) at most 16 rows name the same one
- event_row: int32 [2048], P('dp'), may hold values from 0 to 255
- text_rows: bfloat16 [4096, 4096], P('dp', 'mp'), may hold values from -6 to 6
- image_rows: bfloat16 [4096, 4096], P('dp', 'mp'), may hold values from -6 to 6
- price: float32 [4096], P('dp'), may hold values from 0.2 to 5
- price_dir: bfloat16 [4096], P('mp'), may hold values from -4 to 4
- norm_gain: bfloat16 [4096], P('mp'), may hold values from 0.5 to 1.5
- w_query: bfloat16 [4096, 2048], P('dp', 'mp'), may hold values from -1 to 1
- w_key: bfloat16 [4096, 2048], P('dp', 'mp'), may hold values from -1 to 1
- w_value: bfloat16 [4096, 2048], P('dp', 'mp'), may hold values from -0.09375 to 0.09375
- cotangent: bfloat16 [2048, 4096], P('dp', 'mp'), may hold values from -6 to 6
Outputs:
- context: bfloat16 [2048, 2048], P('dp', 'mp')
- text_grad: float32 [4096, 4096], P('dp', 'mp')
- image_grad: float32 [4096, 4096], P('dp', 'mp')
The draws below stay inside these ranges and needn't reach their ends.
Inputs may be any that keep to these rules, and one draw needn't show every extreme that they name: `event_owner`: among the event slots of one index of dp, no owner is named more than 16 times, a bound that some block reaches.
All inputs are finite; a program needn't handle non-finite values.
Results may differ from the reference program's by a relative error of at most 0.0063.
Values may be sent and summed in bfloat16 or wider, within the bound.
A program may use at most 64 MiB of HBM per device.

```python
import math
import jax
import jax.numpy as jnp
import numpy as np
from jax import lax

D = 4096
HEADS = 16
HD = 128
SLOT = 128
ITEMS_DEV = 256
QW = 2048
TOK_DEV = 128
SESSIONS = 16
TOKENS = 2048
ITEMS = 4096
CAP = 16
N_DP = 16


def projection_parts(key):
    base_part = jax.random.normal(jax.random.fold_in(key, 11), (D, HEADS * HD), jnp.float32) / math.sqrt(D)
    other_part = jax.random.normal(jax.random.fold_in(key, 12), (D, HEADS * HD), jnp.float32) / math.sqrt(D)
    return (base_part, other_part)


def draw_w_query(key, part):
    base_part, other_part = projection_parts(key)
    return jnp.clip(base_part, -1.0, 1.0).astype(jnp.bfloat16)


def draw_w_key(key, part):
    base_part, other_part = projection_parts(key)
    return jnp.clip(other_part, -1.0, 1.0).astype(jnp.bfloat16)


def place_ends(drawn, own_key, smallest, high):
    longest = drawn.shape.index(max(drawn.shape))
    spots = []
    for shift in (0, 1):
        where = [jax.random.randint(jax.random.fold_in(own_key, axis), (), 0, length) for axis, length in enumerate(drawn.shape)]
        where[longest] = (where[longest] + shift) % drawn.shape[longest]
        spots.append(tuple(where))
    return drawn.at[spots[0]].set(smallest).at[spots[1]].set(high)


def shard_levels(key, dims, pieces, smallest, largest):
    def one(axis_at, shards_of):
        heights = jax.random.uniform(jax.random.fold_in(jax.random.fold_in(key, 6), axis_at), (shards_of,), jnp.float32, smallest / len(pieces), largest / len(pieces))
        return jnp.repeat(jnp.exp(heights), dims[axis_at] // shards_of).reshape((-1,) + (1,) * (len(dims) - axis_at - 1))

    factor_of = one(*pieces[0])
    for cut in pieces[1:]:
        factor_of = factor_of * one(*cut)
    return factor_of


def assign_block(own_key, own, number, rows, count, top, most, slope):
    sequence = jax.random.permutation(own_key, count)
    heavy_load, ordinary = load_shares(count, rows * top, most, slope, True), load_shares(count, rows * top, most, slope, False)
    places = jnp.arange(count)

    def named(lengths, turn):
        used = int((lengths > 0).sum())
        fixed = max(1, used // 4)
        passed = fixed + (places - fixed + turn * (used - fixed)) % max(1, count - fixed)
        return jnp.zeros((count,), jnp.int32).at[sequence[jnp.where(places < fixed, places, passed)]].set(jnp.asarray(lengths, jnp.int32))

    lengths = jnp.where(number % 4 == 0, named(heavy_load, number // 4), named(ordinary, number - number // 4 - 1))
    mixed = jax.random.permutation(jax.random.fold_in(own, 3), count)
    donor, receiver = mixed[0:count // 2 * 2:2], mixed[1:count // 2 * 2:2]
    slack = jnp.minimum(lengths[donor] - 1, most - lengths[receiver]) // 2
    slack = jnp.where((donor == sequence[0]) | (receiver == sequence[0]) | (lengths[receiver] == 0), 0, jnp.maximum(slack, 0))
    passed = jax.random.randint(jax.random.fold_in(own, 4), (count // 2,), 0, 1 << 20) % (slack + 1)
    lengths = lengths.at[donor].add(-passed).at[receiver].add(passed)
    members = jnp.searchsorted(jnp.cumsum(lengths), jnp.arange(rows * top), side="right").astype(jnp.int32)
    listing = members.reshape(top, rows).T
    listing = listing[jax.random.permutation(jax.random.fold_in(own, 1), rows)]
    turn = jax.random.randint(jax.random.fold_in(own, 2), (rows, 1), 0, top)
    return jnp.take_along_axis(listing, (jnp.arange(top)[None, :] + turn) % top, axis=1)


def load_shares(count, total, most, skew, full):
    weights = [(1 << 20) // math.isqrt(rank ** skew) + 1 for rank in range(1, count + 1)]
    largest = most if full else min(most, max(-(-total // count), total * weights[0] // sum(weights)))
    least = 1 if total - largest >= count - 1 else 0
    given, rest = [largest] + [least] * (count - 1), total - largest - least * (count - 1)
    while rest > 0:
        movable = [i for i in range(1, count) if given[i] < largest] or [i for i in range(1, count) if given[i] < most]
        pool, left = sum([weights[i] for i in movable]), rest
        for i in movable:
            more = min(most - given[i], max(1, left * weights[i] // pool), rest)
            given[i] = given[i] + more
            rest = rest - more
    return np.array(given)


def noise(rng, dims, deviation, most, pieces=(), kind=jnp.bfloat16):
    values = deviation * jax.random.normal(rng, dims, jnp.float32)
    if pieces:
        values = values * shard_levels(rng, dims, pieces, -0.22, 0.18)
    return jnp.clip(values, -most, most).astype(kind)


def setup_inputs(seed: int = 0) -> dict:
    splits = jax.random.split(jax.random.key(seed), 13)
    session_length = place_ends(jax.random.randint(splits[0], (SESSIONS,), 1, SLOT + 1), jax.random.fold_in(splits[0], 1), 1, SLOT).astype(jnp.int32)
    event_owner_keys = jax.random.split(jax.random.fold_in(splits[1], 1), TOKENS // TOK_DEV)
    event_owner_turns = jax.random.permutation(jax.random.fold_in(splits[1], 3), TOKENS // TOK_DEV)
    event_owner = jax.vmap(lambda own, number: assign_block(jax.random.fold_in(splits[1], 2), own, number, TOK_DEV, N_DP, 1, CAP, 2))(event_owner_keys, event_owner_turns).reshape((TOKENS, 1))
    event_row = place_ends(jax.random.randint(splits[2], (TOKENS,), 0, ITEMS_DEV), jax.random.fold_in(splits[2], 1), 0, ITEMS_DEV - 1).astype(jnp.int32)
    text_rows = noise(splits[3], (ITEMS, D), 1.0, 6.0, ((0, 16), (1, 2)))
    image_rows = noise(splits[4], (ITEMS, D), 1.0, 6.0, ((0, 16), (1, 2)))
    price = jnp.clip(jnp.exp(math.log(5.0) - 3.218876 * jax.random.uniform(splits[5], (ITEMS,), jnp.float32) ** shard_levels(splits[5], (ITEMS,), ((0, 16),), -0.2, 0.2)), 0.2, 5.0)
    price_dir = noise(splits[6], (D,), 1.0, 4.0, ((0, 2),))
    norm_gain = jnp.clip(1.0 + 0.1 * jax.random.normal(splits[7], (D,), jnp.float32), 0.5, 1.5).astype(jnp.bfloat16)
    w_query = draw_w_query(jax.random.fold_in(splits[12], 71), 0)
    w_key = draw_w_key(jax.random.fold_in(splits[12], 71), 0)
    w_value = noise(splits[10], (D, QW), D ** -0.5, 0.09375, ((0, 16), (1, 2)))
    cotangent = noise(splits[11], (TOKENS, D), 1.0, 6.0, ((0, 16), (1, 2)))
    return {"session_length": session_length, "event_owner": event_owner, "event_row": event_row, "text_rows": text_rows, "image_rows": image_rows, "price": price, "price_dir": price_dir, "norm_gain": norm_gain, "w_query": w_query, "w_key": w_key, "w_value": w_value, "cotangent": cotangent}


def one_session(session_args, text_rows, image_rows, price, price_dir, norm_gain, w_query, w_key, w_value):
    items, length = session_args
    text_got = text_rows[items].astype(jnp.float32)
    image_got = image_rows[items].astype(jnp.float32)
    joined_rows = (text_got * image_got + price[items][:, None] * price_dir.astype(jnp.float32)[None, :]).astype(jnp.bfloat16)
    joined_float = joined_rows.astype(jnp.float32)
    scale = lax.rsqrt(lax.optimization_barrier(jnp.mean(joined_float * joined_float, axis=1, keepdims=True)) + 1e-06)
    normed = (joined_float * scale * norm_gain.astype(jnp.float32)[None, :]).astype(jnp.bfloat16)
    query = jnp.dot(normed, w_query, preferred_element_type=jnp.float32).astype(jnp.bfloat16)
    keys = jnp.dot(normed, w_key, preferred_element_type=jnp.float32).astype(jnp.bfloat16)
    values = jnp.dot(normed, w_value, preferred_element_type=jnp.float32).astype(jnp.bfloat16)
    shape3 = (SLOT, HEADS, HD)
    scores = jnp.einsum('qhd,khd->hqk', query.reshape(shape3).astype(jnp.float32), keys.reshape(shape3).astype(jnp.float32)) / math.sqrt(HD)
    position = jnp.arange(SLOT, dtype=jnp.int32)
    live_mask = position < length
    allowed = (position[None, :] <= position[:, None])[None, :, :] & live_mask[None, None, :]
    scores = jnp.where(allowed, scores, jnp.float32(-1e+30))
    row_max = lax.optimization_barrier(jnp.max(scores, axis=-1, keepdims=True))
    powers = jnp.exp(scores - row_max)
    probs = (powers / lax.optimization_barrier(jnp.sum(powers, axis=-1, keepdims=True))).astype(jnp.bfloat16)
    context = jnp.einsum('hqk,khd->qhd', probs.astype(jnp.float32), values.reshape(shape3).astype(jnp.float32))
    context = jnp.where(live_mask[:, None, None], context, jnp.float32(0.0))
    return context.reshape(SLOT, HEADS * HD).astype(jnp.bfloat16)

def reference(session_length, event_owner, event_row, text_rows, image_rows, price, price_dir, norm_gain, w_query, w_key, w_value, cotangent):
    item = (event_owner[:, 0] * ITEMS_DEV + event_row).astype(jnp.int32)

    def per_session(session_args):
        return one_session(session_args, text_rows, image_rows, price, price_dir, norm_gain, w_query, w_key, w_value)
    context = lax.map(per_session, (item.reshape(SESSIONS, SLOT), session_length))
    context = context.reshape(TOKENS, HEADS * HD)
    grad_float = cotangent.astype(jnp.float32)
    text_grad = jnp.zeros((ITEMS, D), jnp.float32).at[item].add(grad_float * image_rows[item].astype(jnp.float32))
    image_grad = jnp.zeros((ITEMS, D), jnp.float32).at[item].add(grad_float * text_rows[item].astype(jnp.float32))
    return (context, text_grad, image_grad)
```

```python
import math

import jax
import jax.numpy as jnp
from jax import lax
from jax.experimental import pallas as pl
from jax.experimental.pallas import tpu as pltpu
from jax.sharding import PartitionSpec as P

D = 4096
HD = 128
SLOT = 128


def fetch_rows(requests, text_rows, image_rows):
    row_ids = jnp.maximum(requests, 0)
    return (row_ids, text_rows[row_ids], image_rows[row_ids])


def join_rows(row_ids, text_got, image_got, price, price_dir):
    price_got = price[row_ids]
    mixed = text_got.astype(jnp.float32) * image_got.astype(jnp.float32) + price_got[
        ..., None
    ] * price_dir.astype(jnp.float32)
    return mixed.astype(jnp.bfloat16)


def answer(requests, text_rows, image_rows, price, price_dir):
    row_ids, text_got, image_got = fetch_rows(requests, text_rows, image_rows)
    joined_rows = join_rows(row_ids, text_got, image_got, price, price_dir)
    replies = lax.all_to_all(joined_rows, "dp", split_axis=0, concat_axis=0, tiled=True)
    return (replies, row_ids, text_got, image_got)


def credit_rows(row_ids, grad_rows, text_got, image_got, table_rows):
    col_width = grad_rows.shape[-1]
    flat_ids = row_ids.reshape(-1)
    grad_float = grad_rows.astype(jnp.float32)
    text_terms = (grad_float * image_got.astype(jnp.float32)).reshape(-1, col_width)
    image_terms = (grad_float * text_got.astype(jnp.float32)).reshape(-1, col_width)
    text_grad = jax.ops.segment_sum(text_terms, flat_ids, num_segments=table_rows)
    image_grad = jax.ops.segment_sum(image_terms, flat_ids, num_segments=table_rows)
    return (text_grad, image_grad)


def attend(query, keys, values, session_length):
    sessions = session_length.shape[0]
    heads_here = query.shape[1] // HD
    shape4 = (sessions, SLOT, heads_here, HD)
    scores = jnp.einsum(
        "sqhd,skhd->shqk",
        query.reshape(shape4),
        keys.reshape(shape4),
        preferred_element_type=jnp.float32,
    ) / math.sqrt(HD)
    position = jnp.arange(SLOT, dtype=jnp.int32)
    live_mask = position[None, :] < session_length[:, None]
    allowed = (position[None, :] <= position[:, None])[None, None, :, :] & live_mask[
        :, None, None, :
    ]
    scores = jnp.where(allowed, scores, jnp.float32(-1e30))
    row_max = jnp.max(scores, axis=-1, keepdims=True)
    powers = jnp.exp(scores - row_max)
    probs = (powers / jnp.sum(powers, axis=-1, keepdims=True)).astype(jnp.bfloat16)
    context = jnp.einsum(
        "shqk,skhd->sqhd", probs, values.reshape(shape4), preferred_element_type=jnp.float32
    )
    context = jnp.where(live_mask[:, :, None, None], context, jnp.float32(0.0))
    return context.reshape(sessions * SLOT, heads_here * HD).astype(jnp.bfloat16)


def local_any(
    session_length,
    event_owner,
    event_row,
    text_rows,
    image_rows,
    price,
    price_dir,
    norm_gain,
    w_query,
    w_key,
    w_value,
    cotangent,
):
    peers = lax.axis_size("dp")
    tok_count = event_row.shape[0]
    capacity = 2 * tok_count // peers
    col_width = text_rows.shape[1]
    table_rows = text_rows.shape[0]
    owner_ids = event_owner[:, 0]
    member = (owner_ids[:, None] == jnp.arange(peers, dtype=jnp.int32)[None, :]).astype(jnp.int32)
    earlier = jnp.sum((jnp.cumsum(member, axis=0) - member) * member, axis=1)
    slot_ids = owner_ids * capacity + earlier
    requests = (
        jnp.full((peers * capacity,), -1, jnp.int32)
        .at[slot_ids]
        .set(event_row)
        .reshape(peers, capacity)
    )
    grad_buffer = (
        jnp.zeros((peers * capacity, col_width), jnp.bfloat16)
        .at[slot_ids]
        .set(cotangent)
        .reshape(peers, capacity, col_width)
    )
    replies = answer(
        lax.all_to_all(requests, "dp", split_axis=0, concat_axis=0, tiled=True),
        text_rows,
        image_rows,
        price,
        price_dir,
    )[0]
    got_ids, got_grads = (
        lax.all_to_all(requests, "dp", split_axis=0, concat_axis=0, tiled=True),
        lax.all_to_all(grad_buffer, "dp", split_axis=0, concat_axis=0, tiled=True),
    )
    row_ids, text_got, image_got = fetch_rows(got_ids, text_rows, image_rows)
    text_grad, image_grad = credit_rows(row_ids, got_grads, text_got, image_got, table_rows)
    joined_rows = replies.reshape(peers * capacity, col_width)[slot_ids]
    joined_float = joined_rows.astype(jnp.float32)
    square_sums = lax.psum(jnp.sum(joined_float * joined_float, axis=1), "mp")
    scale = lax.rsqrt(square_sums / D + 1e-06)
    normed = (joined_float * scale[:, None] * norm_gain.astype(jnp.float32)[None, :]).astype(
        jnp.bfloat16
    )
    features_all = lax.all_gather(normed, "mp", axis=1, tiled=True)

    def add_rows(weight_rows):
        return jnp.dot(features_all, weight_rows, preferred_element_type=jnp.float32)

    query_sum = add_rows(lax.all_gather(w_query, "dp", axis=0, tiled=True))
    key_sum = add_rows(lax.all_gather(w_key, "dp", axis=0, tiled=True))
    value_sum = add_rows(lax.all_gather(w_value, "dp", axis=0, tiled=True))
    context = attend(
        query_sum.astype(jnp.bfloat16),
        key_sum.astype(jnp.bfloat16),
        value_sum.astype(jnp.bfloat16),
        session_length,
    )
    return (context, text_grad, image_grad)


def flip(index, bit):
    return index + bit - 2 * bit * ((index // bit) % 2)


def exchange_kernel(
    reqs_ref, small_ref, price_ref, dir_ref, gain_ref, text_ref, image_ref, cot_ref,
    wq_ref, wk_ref, wv_ref,
    ctx_ref, gsum_ref,
    ids, rep_out, rep_in, grad_out, grad_in, wbuf, xfull, xpart, xown, xsend, part_own,
    part_out, part_in,
    load_sem, id_s, id_r, rep_s, rep_r, grad_s, grad_r, w_s, w_r, y_s, y_r, x_s, x_r, p_s, p_r,
):
    me = lax.axis_index("dp")
    my_y = lax.axis_index("mp")
    n = 16
    cap = 16
    rel = me % 8
    half = me // 8
    wrows = wq_ref.shape[0]
    qw = wq_ref.shape[1]
    loads = [
        pltpu.make_async_copy(w, wbuf.at[k, pl.ds(rel * wrows, wrows), :], load_sem.at[k])
        for k, w in enumerate((wq_ref, wk_ref, wv_ref))
    ]
    for load in loads:
        load.start()
    barrier = pltpu.get_barrier_semaphore()

    def greet(i, carry):
        pl.semaphore_signal(
            barrier, inc=1, device_id={"dp": (me + i) % n}, device_id_type=pl.DeviceIdType.MESH
        )
        return carry

    lax.fori_loop(1, n, greet, 0)
    pl.semaphore_signal(
        barrier, inc=1, device_id={"mp": 1 - my_y}, device_id_type=pl.DeviceIdType.MESH
    )
    pl.semaphore_wait(barrier, n)

    def remote(src, dst, send, recv, **to):
        return pltpu.make_async_remote_copy(
            src_ref=src, dst_ref=dst, send_sem=send, recv_sem=recv, device_id=to,
            device_id_type=pl.DeviceIdType.MESH,
        )

    def swap(src, dst, send, recv):
        def one(i):
            peer = (me + i) % n
            return remote(
                src.at[pl.ds(peer * cap, cap), :], dst.at[pl.ds(me * cap, cap), :],
                send.at[i], recv.at[i], dp=peer,
            )

        def start(i, carry):
            one(i).start()
            return carry

        def finish(i, carry):
            one(i).wait_send()
            one(i).wait_recv()
            return carry

        return (
            lambda: lax.fori_loop(1, n, start, 0),
            lambda: lax.fori_loop(1, n, finish, 0),
        )

    mine = pl.ds(me * cap, cap)
    id_start, id_finish = swap(reqs_ref, ids, id_s, id_r)
    id_start()
    ids[mine, :] = reqs_ref[mine, :]

    def shard(rel_index, low=0, count=wrows):
        return wbuf.at[:, pl.ds(rel_index * wrows + low, count), :]

    def send_w(k, rel_index, bit, low=0, count=wrows):
        block = shard(rel_index, low, count)
        return remote(block, block, w_s.at[k], w_r.at[k], dp=flip(me, bit))

    for load in loads:
        load.wait()
    own_x, own_z, own_c = send_w(0, rel, 2), send_w(1, rel, 4), send_w(2, rel, 1)
    own_x.start()
    own_z.start()
    own_c.start()

    slot = small_ref[0:1, :]
    pick = (
        lax.broadcasted_iota(jnp.int32, (n * cap, SLOT), 0) == slot
    ).astype(jnp.float32).astype(jnp.bfloat16)
    tile = 512
    tiles = text_ref.shape[1] // tile

    def column(j):
        return pl.ds(pl.multiple_of(j * tile, tile), tile)

    def pack_grads(j, carry):
        at = column(j)
        grad_out[:, at] = jnp.dot(
            pick, cot_ref[:, at], preferred_element_type=jnp.float32
        ).astype(jnp.bfloat16)
        return carry

    lax.fori_loop(0, tiles, pack_grads, 0)
    id_finish()
    got = ids[...]
    lane = lax.broadcasted_iota(jnp.int32, got.shape, 1)
    table = text_ref.shape[0]
    want = jnp.concatenate(
        [(got == lane + 128 * k).astype(jnp.float32) for k in range(table // 128)], axis=1
    ).astype(jnp.bfloat16)
    price = price_ref[...]

    def reply(j, carry):
        at = column(j)
        mixed = text_ref[:, at].astype(jnp.float32) * image_ref[:, at].astype(
            jnp.float32
        ) + price * dir_ref[:, at].astype(jnp.float32)
        rep_out[:, at] = jnp.dot(
            want, mixed.astype(jnp.bfloat16), preferred_element_type=jnp.float32
        ).astype(jnp.bfloat16)
        return carry

    lax.fori_loop(0, tiles, reply, 0)
    rep_start, rep_finish = swap(rep_out, rep_in, rep_s, rep_r)
    rep_start()
    rep_in[mine, :] = rep_out[mine, :]
    rep_finish()

    def unpack(j, carry):
        at = column(j)
        xfull[my_y, 0:SLOT, at] = lax.dot_general(
            pick, rep_in[:, at], (((0,), (0,)), ((), ())), preferred_element_type=jnp.float32
        ).astype(jnp.bfloat16)
        xfull[my_y, SLOT : SLOT + 16, at] = jnp.broadcast_to(
            gain_ref[:, at].astype(jnp.float32), (16, tile)
        ).astype(jnp.bfloat16)
        return carry

    lax.fori_loop(0, tiles, unpack, 0)
    across = remote(xfull.at[my_y], xfull.at[my_y], y_s, y_r, mp=1 - my_y)
    across.start()
    grad_start, grad_finish = swap(grad_out, grad_in, grad_s, grad_r)
    grad_start()
    grad_in[mine, :] = grad_out[mine, :]

    hrows = wrows // 2
    own_x.wait_recv()
    x_on = send_w(3, flip(rel, 2), 4, 0, hrows)
    x_on.start()
    x_core = send_w(4, flip(rel, 2), 1)
    x_core.start()
    own_z.wait_recv()
    z_on = send_w(5, flip(rel, 4), 2, hrows, hrows)
    z_on.start()
    z_core = send_w(6, flip(rel, 4), 1)
    z_core.start()

    across.wait_send()
    across.wait_recv()

    def squares(j, total):
        at = column(j)
        a = xfull[0, 0:SLOT, at].astype(jnp.float32)
        b = xfull[1, 0:SLOT, at].astype(jnp.float32)
        return total + jnp.sum(a * a, axis=1, keepdims=True) + jnp.sum(
            b * b, axis=1, keepdims=True
        )

    square_sums = lax.fori_loop(0, tiles, squares, jnp.zeros((SLOT, 1), jnp.float32))
    scale = lax.rsqrt(square_sums / D + 1e-06)

    def normed_at(h, at):
        return (
            xfull[h, 0:SLOT, at].astype(jnp.float32)
            * scale
            * xfull[h, SLOT : SLOT + 1, at].astype(jnp.float32)
        ).astype(jnp.bfloat16)

    def norm_far(j, carry):
        at = column(j)
        xsend[:, at] = normed_at(1 - half, at)
        return carry

    def norm_near(j, carry):
        at = column(j)
        xown[:, at] = normed_at(half, at)
        return carry

    lax.fori_loop(0, tiles, norm_far, 0)
    far = flip(me, 8)
    rows_out = remote(xsend, xpart, x_s, x_r, dp=far)
    rows_out.start()
    lax.fori_loop(0, tiles, norm_near, 0)

    x_on.wait_recv()
    z_on.wait_recv()
    diag_core = send_w(7, flip(flip(rel, 2), 4), 1)
    diag_core.start()
    own_c.wait_recv()
    x_core.wait_recv()
    z_core.wait_recv()
    rows_out.wait_send()
    rows_out.wait_recv()
    diag_core.wait_recv()

    wide = 256
    sends = []
    for k in range(3):

        def project(j, carry, k=k):
            at = pl.ds(pl.multiple_of(j * wide, wide), wide)
            weights = wbuf[k, :, at]
            both = jnp.dot(
                jnp.concatenate([xpart[...], xown[...]], axis=0),
                weights,
                preferred_element_type=jnp.float32,
            )
            part_out[k, :, at] = both[:SLOT].astype(jnp.bfloat16)
            part_own[k, :, at] = both[SLOT:]
            return carry

        lax.fori_loop(0, qw // wide, project, 0)
        send = remote(part_out.at[k], part_in.at[k], p_s.at[k], p_r.at[k], dp=far)
        send.start()
        sends.append(send)

    grad_finish()

    def credit(j, carry):
        at = column(j)
        gsum_ref[:, at] = lax.dot_general(
            want, grad_in[:, at], (((0,), (0,)), ((), ())), preferred_element_type=jnp.float32
        )
        return carry

    lax.fori_loop(0, tiles, credit, 0)
    for copy in (own_x, own_z, own_c, x_on, x_core, z_on, z_core, diag_core):
        copy.wait_send()
    for send in sends:
        send.wait_send()
        send.wait_recv()

    length = small_ref[8:9, :]
    key_at = lax.broadcasted_iota(jnp.int32, (SLOT, SLOT), 1)
    query_at = lax.broadcasted_iota(jnp.int32, (SLOT, SLOT), 0)
    allowed = (key_at <= query_at) & (key_at < length)
    live = query_at < length

    def head(h, carry):
        at = pl.ds(pl.multiple_of(h * HD, HD), HD)
        query, keys, values = [
            (part_own[k, :, at] + part_in[k, :, at].astype(jnp.float32)).astype(jnp.bfloat16)
            for k in range(3)
        ]
        scores = lax.dot_general(
            query, keys, (((1,), (1,)), ((), ())), preferred_element_type=jnp.float32
        ) / math.sqrt(HD)
        scores = jnp.where(allowed, scores, jnp.float32(-1e30))
        powers = jnp.exp(scores - jnp.max(scores, axis=-1, keepdims=True))
        probs = (powers / jnp.sum(powers, axis=-1, keepdims=True)).astype(jnp.bfloat16)
        context = jnp.dot(probs, values, preferred_element_type=jnp.float32)
        ctx_ref[:, at] = jnp.where(live, context, jnp.float32(0.0)).astype(jnp.bfloat16)
        return carry

    lax.fori_loop(0, qw // HD, head, 0)


def local_16(
    session_length, event_owner, event_row, text_rows, image_rows, price, price_dir, norm_gain,
    w_query, w_key, w_value, cotangent,
):
    n = 16
    cap = 16
    tokens = event_row.shape[0]
    width = text_rows.shape[1]
    table = text_rows.shape[0]
    wrows, qw = w_query.shape
    owner_ids = event_owner[:, 0]
    order = jnp.arange(tokens, dtype=jnp.int32)
    earlier = jnp.sum(
        ((owner_ids[:, None] == owner_ids[None, :]) & (order[:, None] < order[None, :])).astype(
            jnp.int32
        ),
        axis=0,
    )
    slot_ids = owner_ids * cap + earlier
    pick = slot_ids[None, :] == jnp.arange(n * cap, dtype=jnp.int32)[:, None]
    asked = jnp.max(jnp.where(pick, event_row[None, :], -1), axis=1)
    reqs = jnp.broadcast_to(asked[:, None], (n * cap, 128))
    small = jnp.concatenate(
        [
            jnp.broadcast_to(slot_ids[None, :], (8, tokens)),
            jnp.broadcast_to(session_length[:, None], (8, tokens)),
        ]
    )
    vmem = pl.BlockSpec(memory_space=pltpu.VMEM)
    hbm = pl.BlockSpec(memory_space=pl.ANY)
    dma = pltpu.SemaphoreType.DMA
    bf16 = jnp.bfloat16
    context, gsum = pl.pallas_call(
        exchange_kernel,
        out_shape=(
            jax.ShapeDtypeStruct((tokens, qw), bf16),
            jax.ShapeDtypeStruct((table, width), jnp.float32),
        ),
        in_specs=[vmem] * 8 + [hbm] * 3,
        out_specs=(vmem, vmem),
        scratch_shapes=[
            pltpu.VMEM((n * cap, 128), jnp.int32),
            pltpu.VMEM((n * cap, width), bf16),
            pltpu.VMEM((n * cap, width), bf16),
            pltpu.VMEM((n * cap, width), bf16),
            pltpu.VMEM((n * cap, width), bf16),
            pltpu.VMEM((3, 8 * wrows, qw), bf16),
            pltpu.VMEM((2, tokens + 16, width), bf16),
            pltpu.VMEM((tokens, width), bf16),
            pltpu.VMEM((tokens, width), bf16),
            pltpu.VMEM((tokens, width), bf16),
            pltpu.VMEM((3, tokens, qw), jnp.float32),
            pltpu.VMEM((3, tokens, qw), bf16),
            pltpu.VMEM((3, tokens, qw), bf16),
            dma((3,)), dma((n,)), dma((n,)), dma((n,)), dma((n,)), dma((n,)), dma((n,)),
            dma((8,)), dma((8,)), dma, dma, dma, dma, dma((3,)), dma((3,)),
        ],
        compiler_params=pltpu.CompilerParams(
            collective_id=0, has_side_effects=True, vmem_limit_bytes=48 * 1024 * 1024
        ),
    )(
        reqs, small, price[:, None], price_dir[None, :], norm_gain[None, :],
        text_rows, image_rows, cotangent, w_query, w_key, w_value,
    )
    text_grad = gsum * image_rows.astype(jnp.float32)
    image_grad = gsum * text_rows.astype(jnp.float32)
    return (context, text_grad, image_grad)


def solution(mesh):
    fits = mesh.shape["dp"] == 16 and mesh.shape["mp"] == 2
    return jax.shard_map(
        local_16 if fits else local_any,
        mesh=mesh,
        in_specs=(
            P("dp"),
            P("dp", None),
            P("dp"),
            P("dp", "mp"),
            P("dp", "mp"),
            P("dp"),
            P("mp"),
            P("mp"),
            P("dp", "mp"),
            P("dp", "mp"),
            P("dp", "mp"),
            P("dp", "mp"),
        ),
        out_specs=(P("dp", "mp"), P("dp", "mp"), P("dp", "mp")),
        check_vma=False,
    )
```

```python
import math

import jax
import jax.numpy as jnp
from jax import lax
from jax.experimental import pallas as pl
from jax.experimental.pallas import tpu as pltpu
from jax.sharding import PartitionSpec as P

D = 4096
HD = 128
SLOT = 128


def fetch_rows(requests, text_rows, image_rows):
    row_ids = jnp.maximum(requests, 0)
    return (row_ids, text_rows[row_ids], image_rows[row_ids])


def join_rows(row_ids, text_got, image_got, price, price_dir):
    price_got = price[row_ids]
    mixed = text_got.astype(jnp.float32) * image_got.astype(jnp.float32) + price_got[
        ..., None
    ] * price_dir.astype(jnp.float32)
    return mixed.astype(jnp.bfloat16)


def answer(requests, text_rows, image_rows, price, price_dir):
    row_ids, text_got, image_got = fetch_rows(requests, text_rows, image_rows)
    joined_rows = join_rows(row_ids, text_got, image_got, price, price_dir)
    replies = lax.all_to_all(joined_rows, "dp", split_axis=0, concat_axis=0, tiled=True)
    return (replies, row_ids, text_got, image_got)


def credit_rows(row_ids, grad_rows, text_got, image_got, table_rows):
    col_width = grad_rows.shape[-1]
    flat_ids = row_ids.reshape(-1)
    grad_float = grad_rows.astype(jnp.float32)
    text_terms = (grad_float * image_got.astype(jnp.float32)).reshape(-1, col_width)
    image_terms = (grad_float * text_got.astype(jnp.float32)).reshape(-1, col_width)
    text_grad = jax.ops.segment_sum(text_terms, flat_ids, num_segments=table_rows)
    image_grad = jax.ops.segment_sum(image_terms, flat_ids, num_segments=table_rows)
    return (text_grad, image_grad)


def attend(query, keys, values, session_length):
    sessions = session_length.shape[0]
    heads_here = query.shape[1] // HD
    shape4 = (sessions, SLOT, heads_here, HD)
    scores = jnp.einsum(
        "sqhd,skhd->shqk",
        query.reshape(shape4),
        keys.reshape(shape4),
        preferred_element_type=jnp.float32,
    ) / math.sqrt(HD)
    position = jnp.arange(SLOT, dtype=jnp.int32)
    live_mask = position[None, :] < session_length[:, None]
    allowed = (position[None, :] <= position[:, None])[None, None, :, :] & live_mask[
        :, None, None, :
    ]
    scores = jnp.where(allowed, scores, jnp.float32(-1e30))
    row_max = jnp.max(scores, axis=-1, keepdims=True)
    powers = jnp.exp(scores - row_max)
    probs = (powers / jnp.sum(powers, axis=-1, keepdims=True)).astype(jnp.bfloat16)
    context = jnp.einsum(
        "shqk,skhd->sqhd", probs, values.reshape(shape4), preferred_element_type=jnp.float32
    )
    context = jnp.where(live_mask[:, :, None, None], context, jnp.float32(0.0))
    return context.reshape(sessions * SLOT, heads_here * HD).astype(jnp.bfloat16)


def local_any(
    session_length,
    event_owner,
    event_row,
    text_rows,
    image_rows,
    price,
    price_dir,
    norm_gain,
    w_query,
    w_key,
    w_value,
    cotangent,
):
    peers = lax.axis_size("dp")
    tok_count = event_row.shape[0]
    capacity = 2 * tok_count // peers
    col_width = text_rows.shape[1]
    table_rows = text_rows.shape[0]
    owner_ids = event_owner[:, 0]
    member = (owner_ids[:, None] == jnp.arange(peers, dtype=jnp.int32)[None, :]).astype(jnp.int32)
    earlier = jnp.sum((jnp.cumsum(member, axis=0) - member) * member, axis=1)
    slot_ids = owner_ids * capacity + earlier
    requests = (
        jnp.full((peers * capacity,), -1, jnp.int32)
        .at[slot_ids]
        .set(event_row)
        .reshape(peers, capacity)
    )
    grad_buffer = (
        jnp.zeros((peers * capacity, col_width), jnp.bfloat16)
        .at[slot_ids]
        .set(cotangent)
        .reshape(peers, capacity, col_width)
    )
    replies = answer(
        lax.all_to_all(requests, "dp", split_axis=0, concat_axis=0, tiled=True),
        text_rows,
        image_rows,
        price,
        price_dir,
    )[0]
    got_ids, got_grads = (
        lax.all_to_all(requests, "dp", split_axis=0, concat_axis=0, tiled=True),
        lax.all_to_all(grad_buffer, "dp", split_axis=0, concat_axis=0, tiled=True),
    )
    row_ids, text_got, image_got = fetch_rows(got_ids, text_rows, image_rows)
    text_grad, image_grad = credit_rows(row_ids, got_grads, text_got, image_got, table_rows)
    joined_rows = replies.reshape(peers * capacity, col_width)[slot_ids]
    joined_float = joined_rows.astype(jnp.float32)
    square_sums = lax.psum(jnp.sum(joined_float * joined_float, axis=1), "mp")
    scale = lax.rsqrt(square_sums / D + 1e-06)
    normed = (joined_float * scale[:, None] * norm_gain.astype(jnp.float32)[None, :]).astype(
        jnp.bfloat16
    )
    features_all = lax.all_gather(normed, "mp", axis=1, tiled=True)

    def add_rows(weight_rows):
        return jnp.dot(features_all, weight_rows, preferred_element_type=jnp.float32)

    query_sum = add_rows(lax.all_gather(w_query, "dp", axis=0, tiled=True))
    key_sum = add_rows(lax.all_gather(w_key, "dp", axis=0, tiled=True))
    value_sum = add_rows(lax.all_gather(w_value, "dp", axis=0, tiled=True))
    context = attend(
        query_sum.astype(jnp.bfloat16),
        key_sum.astype(jnp.bfloat16),
        value_sum.astype(jnp.bfloat16),
        session_length,
    )
    return (context, text_grad, image_grad)


def flip(index, bit):
    return index + bit - 2 * bit * ((index // bit) % 2)


def exchange_kernel(
    reqs_ref, small_ref, price_ref, dir_ref, gain_ref, text_hbm, image_hbm, cot_hbm,
    wq_ref, wk_ref, wv_ref,
    ctx_ref, gsum_ref,
    text_ref, image_ref, cot_ref, ids, slots, tq, tsend, rep_out, rep_in, grad_out, grad_in,
    wbuf, xfull, xin, ss_out, ss_in, part_own, part_out, part_in,
    load_sem, id_s, id_r, rep_s, rep_r, grad_s, grad_r, w_s, w_r, one_s, one_r, p_s, p_r,
):
    me = lax.axis_index("dp")
    my_y = lax.axis_index("mp")
    n = 16
    cap = 16
    rel = me % 8
    half = me // 8
    far = flip(me, 8)
    wrows = wq_ref.shape[0]
    qw = wq_ref.shape[1]
    quarter = dir_ref.shape[1] // 2
    table = text_ref.shape[0]
    both_rows = 2 * SLOT
    weights_in = (wq_ref, wk_ref, wv_ref)
    table_loads = [
        pltpu.make_async_copy(a, b, load_sem.at[3 + k])
        for k, (a, b) in enumerate(
            ((text_hbm, text_ref), (image_hbm, image_ref), (cot_hbm, cot_ref))
        )
    ]
    w_loads = [
        pltpu.make_async_copy(w, wbuf.at[k, pl.ds(rel * wrows, wrows), :], load_sem.at[k])
        for k, w in enumerate(weights_in)
    ]
    for load in table_loads[:2] + w_loads + table_loads[2:]:
        load.start()
    barrier = pltpu.get_barrier_semaphore()

    def greet(i, carry):
        pl.semaphore_signal(
            barrier, inc=1, device_id={"dp": (me + i) % n}, device_id_type=pl.DeviceIdType.MESH
        )
        return carry

    lax.fori_loop(1, n, greet, 0)
    pl.semaphore_signal(
        barrier, inc=1, device_id={"mp": 1 - my_y}, device_id_type=pl.DeviceIdType.MESH
    )
    pl.semaphore_signal(
        barrier, inc=1, device_id={"dp": far, "mp": 1 - my_y},
        device_id_type=pl.DeviceIdType.MESH,
    )
    pl.semaphore_wait(barrier, n + 1)

    def remote(src, dst, send, recv, **to):
        return pltpu.make_async_remote_copy(
            src_ref=src, dst_ref=dst, send_sem=send, recv_sem=recv, device_id=to,
            device_id_type=pl.DeviceIdType.MESH,
        )

    def swap(src_of, dst, send, recv):
        def one(i):
            peer = (me + i) % n
            return remote(src_of(peer), dst, send.at[i], recv.at[i], dp=peer)

        def start(i, carry):
            one(i).start()
            return carry

        def finish(i, carry):
            one(i).wait_send()
            one(i).wait_recv()
            return carry

        return (
            lambda: lax.fori_loop(1, n, start, 0),
            lambda: lax.fori_loop(1, n, finish, 0),
        )

    def block(peer):
        return pl.ds(peer * cap, cap)

    id_start, id_finish = swap(
        lambda p: reqs_ref.at[block(p), :], ids.at[block(me), :], id_s, id_r
    )
    id_start()
    slots[half] = small_ref[0:8, :]
    slot_out = remote(
        small_ref.at[pl.ds(0, 8), :], slots.at[half], one_s.at[0], one_r.at[0], dp=far
    )
    slot_out.start()
    ids[block(me), :] = reqs_ref[block(me), :]

    def send_w(k, c, rel_index, bit, low=0, count=wrows):
        part = wbuf.at[k, pl.ds(rel_index * wrows + low, count), :]
        return remote(part, part, w_s.at[8 * k + c], w_r.at[8 * k + c], dp=flip(me, bit))

    hrows = wrows // 2
    own_x = [send_w(k, 0, rel, 2) for k in range(3)]
    own_z = [send_w(k, 1, rel, 4) for k in range(3)]
    own_c = [send_w(k, 2, rel, 1) for k in range(3)]
    x_on = [send_w(k, 3, flip(rel, 2), 4, 0, hrows) for k in range(3)]
    x_core = [send_w(k, 4, flip(rel, 2), 1) for k in range(3)]
    z_on = [send_w(k, 5, flip(rel, 4), 2, hrows, hrows) for k in range(3)]
    z_core = [send_w(k, 6, flip(rel, 4), 1) for k in range(3)]
    diag_core = [send_w(k, 7, flip(flip(rel, 2), 4), 1) for k in range(3)]

    def pass_on(k):
        own_x[k].wait_recv()
        x_on[k].start()
        x_core[k].start()
        own_z[k].wait_recv()
        z_on[k].start()
        z_core[k].start()

    def pass_diag(k):
        x_on[k].wait_recv()
        z_on[k].wait_recv()
        diag_core[k].start()

    table_loads[0].wait()
    table_loads[1].wait()
    tile = 512
    tiles = quarter // tile
    price = price_ref[...]

    def join(start, j):
        src = pl.ds(pl.multiple_of(start + j * tile, tile), tile)
        mixed = text_ref[:, src].astype(jnp.float32) * image_ref[:, src].astype(
            jnp.float32
        ) + price * dir_ref[:, src].astype(jnp.float32)
        gain = jnp.broadcast_to(gain_ref[:, src].astype(jnp.float32), (16, tile))
        return mixed.astype(jnp.bfloat16), gain.astype(jnp.bfloat16)

    def column(j):
        return pl.ds(pl.multiple_of(j * tile, tile), tile)

    def join_out(j, carry):
        rows, gain = join((1 - my_y) * quarter, j)
        tsend[0:table, column(j)] = rows
        tsend[table : table + 16, column(j)] = gain
        return carry

    def join_own(j, carry):
        rows, gain = join(my_y * quarter, j)
        tq[my_y, 0:table, column(j)] = rows
        tq[my_y, table : table + 16, column(j)] = gain
        return carry

    lax.fori_loop(0, tiles, join_out, 0)
    table_out = remote(tsend, tq.at[my_y], one_s.at[1], one_r.at[1], mp=1 - my_y)
    table_out.start()
    for k in range(3):
        w_loads[k].wait()
        own_x[k].start()
        own_z[k].start()
        own_c[k].start()
    lax.fori_loop(0, tiles, join_own, 0)

    def pick_of(slot):
        return (
            lax.broadcasted_iota(jnp.int32, (n * cap, SLOT), 0) == slot
        ).astype(jnp.float32).astype(jnp.bfloat16)

    id_finish()
    got = ids[...]
    lane = lax.broadcasted_iota(jnp.int32, got.shape, 1)
    want = jnp.concatenate(
        [(got == lane + 128 * k).astype(jnp.float32) for k in range(table // 128)], axis=1
    ).astype(jnp.bfloat16)
    table_out.wait_send()
    table_out.wait_recv()
    for m in range(2):

        def reply(j, carry, m=m):
            rows = jnp.dot(
                want, tq[m, 0:table, column(j)], preferred_element_type=jnp.float32
            ).astype(jnp.bfloat16)
            rep_out[m, 0, :, column(j)] = rows[: 8 * cap]
            rep_out[m, 1, :, column(j)] = rows[8 * cap :]
            return carry

        lax.fori_loop(0, tiles, reply, 0)
    rep_start, rep_finish = swap(
        lambda p: rep_out.at[p // 8, :, block(p % 8), :], rep_in.at[:, block(me), :],
        rep_s, rep_r,
    )
    rep_start()
    rep_in[:, block(me), :] = rep_out[half, :, block(rel), :]
    table_loads[2].wait()
    pick = pick_of(small_ref[0:1, :])

    def pack_grads(j, carry):
        grad_out[:, column(j)] = jnp.dot(
            pick, cot_ref[:, column(j)], preferred_element_type=jnp.float32
        ).astype(jnp.bfloat16)
        return carry

    lax.fori_loop(0, 2 * tiles, pack_grads, 0)
    pass_on(0)
    slot_out.wait_send()
    slot_out.wait_recv()
    rep_finish()

    for zs in range(2):
        chosen = pick_of(slots[zs, 0:1, :])

        def unpack(j, carry, zs=zs, chosen=chosen):
            xfull[my_y, zs * SLOT : (zs + 1) * SLOT, column(j)] = lax.dot_general(
                chosen, rep_in[zs, :, column(j)], (((0,), (0,)), ((), ())),
                preferred_element_type=jnp.float32,
            ).astype(jnp.bfloat16)
            return carry

        lax.fori_loop(0, tiles, unpack, 0)
    xfull[my_y, both_rows : both_rows + 16, :] = tq[half, table : table + 16, :]
    across = remote(xfull.at[my_y], xfull.at[my_y], one_s.at[2], one_r.at[2], mp=1 - my_y)
    across.start()

    def squares(q):
        def add(j, total):
            a = xfull[q, 0:both_rows, column(j)].astype(jnp.float32)
            return total + jnp.sum(a * a, axis=1, keepdims=True)

        return lax.fori_loop(0, tiles, add, jnp.zeros((both_rows, 1), jnp.float32))

    near = squares(my_y)
    ss_out[...] = jnp.transpose(jnp.broadcast_to(near, (both_rows, 128)))[0:8, :]
    ss_far = remote(ss_out, ss_in.at[0], one_s.at[3], one_r.at[3], dp=far)
    ss_far.start()
    ss_diag = remote(ss_out, ss_in.at[1], one_s.at[4], one_r.at[4], dp=far, mp=1 - my_y)
    ss_diag.start()
    pass_on(1)
    pass_diag(0)
    pass_on(2)
    grad_start, grad_finish = swap(
        lambda p: grad_out.at[block(p), :], grad_in.at[block(me), :], grad_s, grad_r
    )
    grad_start()
    grad_in[block(me), :] = grad_out[block(me), :]
    across.wait_send()
    across.wait_recv()
    near = near + squares(1 - my_y)
    for copy in (ss_far, ss_diag):
        copy.wait_send()
        copy.wait_recv()
    beyond = ss_in[0] + ss_in[1]
    beyond = jnp.transpose(jnp.broadcast_to(beyond[0:1, :], (128, both_rows)))[:, 0:1]
    scale = lax.rsqrt((near + beyond) / D + 1e-06)
    for q in range(2):

        def norm(j, carry, q=q):
            normed = (
                xfull[q, 0:both_rows, column(j)].astype(jnp.float32)
                * scale
                * xfull[q, both_rows : both_rows + 1, column(j)].astype(jnp.float32)
            )
            xin[:, column(q * tiles + j)] = normed.astype(jnp.bfloat16)
            return carry

        lax.fori_loop(0, tiles, norm, 0)

    wide = 256
    sends = []
    for k in range(3):
        if k:
            pass_diag(k)
        own_c[k].wait_recv()
        x_core[k].wait_recv()
        z_core[k].wait_recv()
        diag_core[k].wait_recv()

        def project(j, carry, k=k):
            at = pl.ds(pl.multiple_of(j * wide, wide), wide)
            both = jnp.dot(xin[...], wbuf[k, :, at], preferred_element_type=jnp.float32)
            for zs in range(2):
                rows = both[zs * SLOT : (zs + 1) * SLOT]
                part_own[k, zs, :, at] = rows
                part_out[k, zs, :, at] = rows.astype(jnp.bfloat16)
            return carry

        lax.fori_loop(0, qw // wide, project, 0)
        send = remote(
            part_out.at[k, 1 - half], part_in.at[k], p_s.at[k], p_r.at[k], dp=far
        )
        send.start()
        sends.append(send)

    grad_finish()

    def credit(j, carry):
        gsum_ref[:, column(j)] = lax.dot_general(
            want, grad_in[:, column(j)], (((0,), (0,)), ((), ())),
            preferred_element_type=jnp.float32,
        )
        return carry

    lax.fori_loop(0, 2 * tiles, credit, 0)
    for group in (own_x, own_z, own_c, x_on, x_core, z_on, z_core, diag_core):
        for copy in group:
            copy.wait_send()
    for send in sends:
        send.wait_send()
        send.wait_recv()

    length = small_ref[8:9, :]
    key_at = lax.broadcasted_iota(jnp.int32, (SLOT, SLOT), 1)
    query_at = lax.broadcasted_iota(jnp.int32, (SLOT, SLOT), 0)
    allowed = (key_at <= query_at) & (key_at < length)
    live = query_at < length

    def head(h, carry):
        at = pl.ds(pl.multiple_of(h * HD, HD), HD)
        query, keys, values = [
            (part_own[k, half, :, at] + part_in[k, :, at].astype(jnp.float32)).astype(
                jnp.bfloat16
            )
            for k in range(3)
        ]
        scores = lax.dot_general(
            query, keys, (((1,), (1,)), ((), ())), preferred_element_type=jnp.float32
        ) / math.sqrt(HD)
        scores = jnp.where(allowed, scores, jnp.float32(-1e30))
        powers = jnp.exp(scores - jnp.max(scores, axis=-1, keepdims=True))
        probs = (powers / jnp.sum(powers, axis=-1, keepdims=True)).astype(jnp.bfloat16)
        context = jnp.dot(probs, values, preferred_element_type=jnp.float32)
        ctx_ref[:, at] = jnp.where(live, context, jnp.float32(0.0)).astype(jnp.bfloat16)
        return carry

    lax.fori_loop(0, qw // HD, head, 0)


def local_16(
    session_length, event_owner, event_row, text_rows, image_rows, price, price_dir, norm_gain,
    w_query, w_key, w_value, cotangent,
):
    n = 16
    cap = 16
    tokens = event_row.shape[0]
    width = text_rows.shape[1]
    table = text_rows.shape[0]
    wrows, qw = w_query.shape
    owner_ids = event_owner[:, 0]
    order = jnp.arange(tokens, dtype=jnp.int32)
    earlier = jnp.sum(
        ((owner_ids[:, None] == owner_ids[None, :]) & (order[:, None] < order[None, :])).astype(
            jnp.int32
        ),
        axis=0,
    )
    slot_ids = owner_ids * cap + earlier
    pick = slot_ids[None, :] == jnp.arange(n * cap, dtype=jnp.int32)[:, None]
    asked = jnp.max(jnp.where(pick, event_row[None, :], -1), axis=1)
    reqs = jnp.broadcast_to(asked[:, None], (n * cap, 128))
    small = jnp.concatenate(
        [
            jnp.broadcast_to(slot_ids[None, :], (8, tokens)),
            jnp.broadcast_to(session_length[:, None], (8, tokens)),
        ]
    )
    vmem = pl.BlockSpec(memory_space=pltpu.VMEM)
    hbm = pl.BlockSpec(memory_space=pl.ANY)
    dma = pltpu.SemaphoreType.DMA
    bf16 = jnp.bfloat16
    context, gsum = pl.pallas_call(
        exchange_kernel,
        out_shape=(
            jax.ShapeDtypeStruct((tokens, qw), bf16),
            jax.ShapeDtypeStruct((table, width), jnp.float32),
        ),
        in_specs=[vmem] * 5 + [hbm] * 6,
        out_specs=(vmem, vmem),
        scratch_shapes=[
            pltpu.VMEM((table, width), bf16),
            pltpu.VMEM((table, width), bf16),
            pltpu.VMEM((tokens, width), bf16),
            pltpu.VMEM((n * cap, 128), jnp.int32),
            pltpu.VMEM((2, 8, tokens), jnp.int32),
            pltpu.VMEM((2, table + 16, width // 2), bf16),
            pltpu.VMEM((table + 16, width // 2), bf16),
            pltpu.VMEM((2, 2, 8 * cap, width // 2), bf16),
            pltpu.VMEM((2, n * cap, width // 2), bf16),
            pltpu.VMEM((n * cap, width), bf16),
            pltpu.VMEM((n * cap, width), bf16),
            pltpu.VMEM((3, 8 * wrows, qw), bf16),
            pltpu.VMEM((2, 2 * tokens + 16, width // 2), bf16),
            pltpu.VMEM((2 * tokens, width), bf16),
            pltpu.VMEM((8, 2 * tokens), jnp.float32),
            pltpu.VMEM((2, 8, 2 * tokens), jnp.float32),
            pltpu.VMEM((3, 2, tokens, qw), jnp.float32),
            pltpu.VMEM((3, 2, tokens, qw), bf16),
            pltpu.VMEM((3, tokens, qw), bf16),
            dma((6,)), dma((n,)), dma((n,)), dma((n,)), dma((n,)), dma((n,)), dma((n,)),
            dma((24,)), dma((24,)), dma((5,)), dma((5,)), dma((3,)), dma((3,)),
        ],
        compiler_params=pltpu.CompilerParams(
            collective_id=0, has_side_effects=True, vmem_limit_bytes=60 * 1024 * 1024
        ),
    )(
        reqs, small, price[:, None], price_dir[None, :], norm_gain[None, :],
        text_rows, image_rows, cotangent, w_query, w_key, w_value,
    )
    text_grad = gsum * image_rows.astype(jnp.float32)
    image_grad = gsum * text_rows.astype(jnp.float32)
    return (context, text_grad, image_grad)


def solution(mesh):
    fits = mesh.shape["dp"] == 16 and mesh.shape["mp"] == 2
    return jax.shard_map(
        local_16 if fits else local_any,
        mesh=mesh,
        in_specs=(
            P("dp"),
            P("dp", None),
            P("dp"),
            P("dp", "mp"),
            P("dp", "mp"),
            P("dp"),
            P("mp"),
            P("mp"),
            P("dp", "mp"),
            P("dp", "mp"),
            P("dp", "mp"),
            P("dp", "mp"),
        ),
        out_specs=(P("dp", "mp"), P("dp", "mp"), P("dp", "mp")),
        check_vma=False,
    )
```

```python
import math

import jax
import jax.numpy as jnp
from jax import lax
from jax.experimental import pallas as pl
from jax.experimental.pallas import tpu as pltpu
from jax.sharding import PartitionSpec as P

D = 4096
HD = 128
SLOT = 128


def fetch_rows(requests, text_rows, image_rows):
    row_ids = jnp.maximum(requests, 0)
    return (row_ids, text_rows[row_ids], image_rows[row_ids])


def join_rows(row_ids, text_got, image_got, price, price_dir):
    price_got = price[row_ids]
    mixed = text_got.astype(jnp.float32) * image_got.astype(jnp.float32) + price_got[
        ..., None
    ] * price_dir.astype(jnp.float32)
    return mixed.astype(jnp.bfloat16)


def answer(requests, text_rows, image_rows, price, price_dir):
    row_ids, text_got, image_got = fetch_rows(requests, text_rows, image_rows)
    joined_rows = join_rows(row_ids, text_got, image_got, price, price_dir)
    replies = lax.all_to_all(joined_rows, "dp", split_axis=0, concat_axis=0, tiled=True)
    return (replies, row_ids, text_got, image_got)


def credit_rows(row_ids, grad_rows, text_got, image_got, table_rows):
    col_width = grad_rows.shape[-1]
    flat_ids = row_ids.reshape(-1)
    grad_float = grad_rows.astype(jnp.float32)
    text_terms = (grad_float * image_got.astype(jnp.float32)).reshape(-1, col_width)
    image_terms = (grad_float * text_got.astype(jnp.float32)).reshape(-1, col_width)
    text_grad = jax.ops.segment_sum(text_terms, flat_ids, num_segments=table_rows)
    image_grad = jax.ops.segment_sum(image_terms, flat_ids, num_segments=table_rows)
    return (text_grad, image_grad)


def attend(query, keys, values, session_length):
    sessions = session_length.shape[0]
    heads_here = query.shape[1] // HD
    shape4 = (sessions, SLOT, heads_here, HD)
    scores = jnp.einsum(
        "sqhd,skhd->shqk",
        query.reshape(shape4),
        keys.reshape(shape4),
        preferred_element_type=jnp.float32,
    ) / math.sqrt(HD)
    position = jnp.arange(SLOT, dtype=jnp.int32)
    live_mask = position[None, :] < session_length[:, None]
    allowed = (position[None, :] <= position[:, None])[None, None, :, :] & live_mask[
        :, None, None, :
    ]
    scores = jnp.where(allowed, scores, jnp.float32(-1e30))
    row_max = jnp.max(scores, axis=-1, keepdims=True)
    powers = jnp.exp(scores - row_max)
    probs = (powers / jnp.sum(powers, axis=-1, keepdims=True)).astype(jnp.bfloat16)
    context = jnp.einsum(
        "shqk,skhd->sqhd", probs, values.reshape(shape4), preferred_element_type=jnp.float32
    )
    context = jnp.where(live_mask[:, :, None, None], context, jnp.float32(0.0))
    return context.reshape(sessions * SLOT, heads_here * HD).astype(jnp.bfloat16)


def local_any(
    session_length,
    event_owner,
    event_row,
    text_rows,
    image_rows,
    price,
    price_dir,
    norm_gain,
    w_query,
    w_key,
    w_value,
    cotangent,
):
    peers = lax.axis_size("dp")
    tok_count = event_row.shape[0]
    capacity = 2 * tok_count // peers
    col_width = text_rows.shape[1]
    table_rows = text_rows.shape[0]
    owner_ids = event_owner[:, 0]
    member = (owner_ids[:, None] == jnp.arange(peers, dtype=jnp.int32)[None, :]).astype(jnp.int32)
    earlier = jnp.sum((jnp.cumsum(member, axis=0) - member) * member, axis=1)
    slot_ids = owner_ids * capacity + earlier
    requests = (
        jnp.full((peers * capacity,), -1, jnp.int32)
        .at[slot_ids]
        .set(event_row)
        .reshape(peers, capacity)
    )
    grad_buffer = (
        jnp.zeros((peers * capacity, col_width), jnp.bfloat16)
        .at[slot_ids]
        .set(cotangent)
        .reshape(peers, capacity, col_width)
    )
    replies = answer(
        lax.all_to_all(requests, "dp", split_axis=0, concat_axis=0, tiled=True),
        text_rows,
        image_rows,
        price,
        price_dir,
    )[0]
    got_ids, got_grads = (
        lax.all_to_all(requests, "dp", split_axis=0, concat_axis=0, tiled=True),
        lax.all_to_all(grad_buffer, "dp", split_axis=0, concat_axis=0, tiled=True),
    )
    row_ids, text_got, image_got = fetch_rows(got_ids, text_rows, image_rows)
    text_grad, image_grad = credit_rows(row_ids, got_grads, text_got, image_got, table_rows)
    joined_rows = replies.reshape(peers * capacity, col_width)[slot_ids]
    joined_float = joined_rows.astype(jnp.float32)
    square_sums = lax.psum(jnp.sum(joined_float * joined_float, axis=1), "mp")
    scale = lax.rsqrt(square_sums / D + 1e-06)
    normed = (joined_float * scale[:, None] * norm_gain.astype(jnp.float32)[None, :]).astype(
        jnp.bfloat16
    )
    features_all = lax.all_gather(normed, "mp", axis=1, tiled=True)

    def add_rows(weight_rows):
        return jnp.dot(features_all, weight_rows, preferred_element_type=jnp.float32)

    query_sum = add_rows(lax.all_gather(w_query, "dp", axis=0, tiled=True))
    key_sum = add_rows(lax.all_gather(w_key, "dp", axis=0, tiled=True))
    value_sum = add_rows(lax.all_gather(w_value, "dp", axis=0, tiled=True))
    context = attend(
        query_sum.astype(jnp.bfloat16),
        key_sum.astype(jnp.bfloat16),
        value_sum.astype(jnp.bfloat16),
        session_length,
    )
    return (context, text_grad, image_grad)


def flip(index, bit):
    return index + bit - 2 * bit * ((index // bit) % 2)


def exchange_kernel(
    length_ref, owner_ref, row_ref, price_ref, dir_ref, gain_ref, text_hbm, image_hbm, cot_hbm,
    wq_ref, wk_ref, wv_ref,
    ctx_ref, gsum_ref,
    text_ref, image_ref, cot_ref, reqs_ref, probs_ref, ids, slots, tq, tsend, rep_out, rep_in, grad_out, grad_in,
    fvals, wbuf, xfull, xin, ss_out, ss_in, part_own, part_out, part_in,
    load_sem, id_s, id_r, rep_s, rep_r, grad_s, grad_r, w_s, w_r, one_s, one_r, p_s, p_r,
):
    me = lax.axis_index("dp")
    my_y = lax.axis_index("mp")
    n = 16
    cap = 16
    rel = me % 8
    half = me // 8
    far = flip(me, 8)
    wrows = wq_ref.shape[0]
    qw = wq_ref.shape[1]
    quarter = dir_ref.shape[0] // 2
    table = text_ref.shape[0]
    both_rows = 2 * SLOT
    weights_in = (wq_ref, wk_ref, wv_ref)
    table_loads = [
        pltpu.make_async_copy(a, b, load_sem.at[3 + k])
        for k, (a, b) in enumerate(
            ((text_hbm, text_ref), (image_hbm, image_ref), (cot_hbm, cot_ref))
        )
    ]
    w_loads = [
        pltpu.make_async_copy(w, wbuf.at[k, pl.ds(rel * wrows, wrows), :], load_sem.at[k])
        for k, w in enumerate(weights_in)
    ]
    for load in w_loads + table_loads:
        load.start()
    def lanes(ref, rows):
        return jnp.broadcast_to(ref[...].reshape(1, ref.shape[0]), (rows, ref.shape[0]))

    owner_along = lanes(owner_ref, SLOT)
    before = lax.broadcasted_iota(jnp.int32, (SLOT, SLOT), 0) < lax.broadcasted_iota(
        jnp.int32, (SLOT, SLOT), 1
    )
    same = (jnp.transpose(owner_along) == owner_along) & before
    slot = owner_along[0:1, :] * cap + jnp.sum(same.astype(jnp.int32), axis=0, keepdims=True)
    picked = lax.broadcasted_iota(jnp.int32, (n * cap, SLOT), 0) == slot
    asked = jnp.max(jnp.where(picked, lanes(row_ref, n * cap), -1), axis=1, keepdims=True)
    reqs_ref[...] = jnp.broadcast_to(asked, (n * cap, 128))
    slots[half] = jnp.broadcast_to(slot, (8, SLOT))
    barrier = pltpu.get_barrier_semaphore()

    def greet(i, carry):
        pl.semaphore_signal(
            barrier, inc=1, device_id={"dp": (me + i) % n}, device_id_type=pl.DeviceIdType.MESH
        )
        return carry

    lax.fori_loop(1, n, greet, 0)
    pl.semaphore_signal(
        barrier, inc=1, device_id={"mp": 1 - my_y}, device_id_type=pl.DeviceIdType.MESH
    )
    pl.semaphore_signal(
        barrier, inc=1, device_id={"dp": far, "mp": 1 - my_y},
        device_id_type=pl.DeviceIdType.MESH,
    )
    pl.semaphore_wait(barrier, n + 1)

    def remote(src, dst, send, recv, **to):
        return pltpu.make_async_remote_copy(
            src_ref=src, dst_ref=dst, send_sem=send, recv_sem=recv, device_id=to,
            device_id_type=pl.DeviceIdType.MESH,
        )

    def swap(src_of, dst, send, recv):
        def one(i):
            peer = (me + i) % n
            return remote(src_of(peer), dst, send.at[i], recv.at[i], dp=peer)

        def start(i, carry):
            one(i).start()
            return carry

        def finish(i, carry):
            one(i).wait_send()
            one(i).wait_recv()
            return carry

        return (
            lambda: lax.fori_loop(1, n, start, 0),
            lambda: lax.fori_loop(1, n, finish, 0),
        )

    def block(peer):
        return pl.ds(peer * cap, cap)

    id_start, id_finish = swap(
        lambda p: reqs_ref.at[block(p), :], ids.at[block(me), :], id_s, id_r
    )
    id_start()
    slot_out = remote(slots.at[half], slots.at[half], one_s.at[0], one_r.at[0], dp=far)
    slot_out.start()
    ids[block(me), :] = reqs_ref[block(me), :]

    def send_w(k, c, rel_index, bit, low=0, count=wrows):
        part = wbuf.at[k, pl.ds(rel_index * wrows + low, count), :]
        return remote(part, part, w_s.at[8 * k + c], w_r.at[8 * k + c], dp=flip(me, bit))

    zrows = wrows // 4
    own_x = [send_w(k, 0, rel, 2) for k in range(3)]
    own_z = [send_w(k, 1, rel, 4) for k in range(3)]
    own_c = [send_w(k, 2, rel, 1) for k in range(3)]
    x_on = [send_w(k, 3, flip(rel, 2), 4, 0, zrows) for k in range(3)]
    x_core = [send_w(k, 4, flip(rel, 2), 1) for k in range(3)]
    z_on = [send_w(k, 5, flip(rel, 4), 2, zrows, wrows - zrows) for k in range(3)]
    z_core = [send_w(k, 6, flip(rel, 4), 1) for k in range(3)]
    diag_core = [send_w(k, 7, flip(flip(rel, 2), 4), 1) for k in range(3)]

    def pass_on(k):
        own_x[k].wait_recv()
        x_on[k].start()
        x_core[k].start()
        own_z[k].wait_recv()
        z_on[k].start()
        z_core[k].start()

    def pass_diag(k):
        x_on[k].wait_recv()
        z_on[k].wait_recv()
        diag_core[k].start()

    for k in range(3):
        w_loads[k].wait()
        own_x[k].start()
        own_z[k].start()
        own_c[k].start()
    table_loads[0].wait()
    table_loads[1].wait()
    tile = 512
    tiles = quarter // tile
    price = jnp.transpose(lanes(price_ref, 128))[:, 0:1]
    dir_row = dir_ref[...].astype(jnp.float32).reshape(1, 2 * quarter)
    gain_row = gain_ref[...].astype(jnp.float32).reshape(1, 2 * quarter)
    fvals[0:1, :] = dir_row
    fvals[8:9, :] = gain_row

    def join(start, j):
        src = pl.ds(pl.multiple_of(start + j * tile, tile), tile)
        mixed = text_ref[:, src].astype(jnp.float32) * image_ref[:, src].astype(
            jnp.float32
        ) + price * fvals[0:1, src]
        gain = jnp.broadcast_to(fvals[8:9, src], (16, tile))
        return mixed.astype(jnp.bfloat16), gain.astype(jnp.bfloat16)

    def column(j):
        return pl.ds(pl.multiple_of(j * tile, tile), tile)

    def join_out(j, carry):
        rows, gain = join((1 - my_y) * quarter, j)
        tsend[0:table, column(j)] = rows
        tsend[table : table + 16, column(j)] = gain
        return carry

    def join_own(j, carry):
        rows, gain = join(my_y * quarter, j)
        tq[my_y, 0:table, column(j)] = rows
        tq[my_y, table : table + 16, column(j)] = gain
        return carry

    lax.fori_loop(0, tiles, join_out, 0)
    table_out = remote(tsend, tq.at[my_y], one_s.at[1], one_r.at[1], mp=1 - my_y)
    table_out.start()
    lax.fori_loop(0, tiles, join_own, 0)

    def pick_of(slot):
        return (
            lax.broadcasted_iota(jnp.int32, (n * cap, SLOT), 0) == slot
        ).astype(jnp.float32).astype(jnp.bfloat16)

    id_finish()
    got = ids[...]
    lane = lax.broadcasted_iota(jnp.int32, got.shape, 1)
    want = jnp.concatenate(
        [(got == lane + 128 * k).astype(jnp.float32) for k in range(table // 128)], axis=1
    ).astype(jnp.bfloat16)
    table_out.wait_send()
    table_out.wait_recv()
    for m in range(2):

        def reply(j, carry, m=m):
            rows = jnp.dot(
                want, tq[m, 0:table, column(j)], preferred_element_type=jnp.float32
            ).astype(jnp.bfloat16)
            rep_out[m, 0, :, column(j)] = rows[: 8 * cap]
            rep_out[m, 1, :, column(j)] = rows[8 * cap :]
            return carry

        lax.fori_loop(0, tiles, reply, 0)
    rep_start, rep_finish = swap(
        lambda p: rep_out.at[p // 8, :, block(p % 8), :], rep_in.at[:, block(me), :],
        rep_s, rep_r,
    )
    rep_start()
    rep_in[:, block(me), :] = rep_out[half, :, block(rel), :]
    table_loads[2].wait()
    pick = pick_of(slots[half, 0:1, :])

    def pack_grads(j, carry):
        grad_out[:, column(j)] = jnp.dot(
            pick, cot_ref[:, column(j)], preferred_element_type=jnp.float32
        ).astype(jnp.bfloat16)
        return carry

    lax.fori_loop(0, 2 * tiles, pack_grads, 0)
    pass_on(0)
    slot_out.wait_send()
    slot_out.wait_recv()
    rep_finish()

    for zs in range(2):
        chosen = pick_of(slots[zs, 0:1, :])

        def unpack(j, carry, zs=zs, chosen=chosen):
            xfull[my_y, zs * SLOT : (zs + 1) * SLOT, column(j)] = lax.dot_general(
                chosen, rep_in[zs, :, column(j)], (((0,), (0,)), ((), ())),
                preferred_element_type=jnp.float32,
            ).astype(jnp.bfloat16)
            return carry

        lax.fori_loop(0, tiles, unpack, 0)
    xfull[my_y, both_rows : both_rows + 16, :] = tq[half, table : table + 16, :]
    across = remote(xfull.at[my_y], xfull.at[my_y], one_s.at[2], one_r.at[2], mp=1 - my_y)
    across.start()

    def squares(q):
        def add(j, total):
            a = xfull[q, 0:both_rows, column(j)].astype(jnp.float32)
            return total + jnp.sum(a * a, axis=1, keepdims=True)

        return lax.fori_loop(0, tiles, add, jnp.zeros((both_rows, 1), jnp.float32))

    near = squares(my_y)
    ss_out[...] = jnp.transpose(jnp.broadcast_to(near, (both_rows, 128)))[0:8, :]
    ss_far = remote(ss_out, ss_in.at[0], one_s.at[3], one_r.at[3], dp=far)
    ss_far.start()
    ss_diag = remote(ss_out, ss_in.at[1], one_s.at[4], one_r.at[4], dp=far, mp=1 - my_y)
    ss_diag.start()
    pass_on(1)
    pass_diag(0)
    pass_on(2)
    grad_start, grad_finish = swap(
        lambda p: grad_out.at[block(p), :], grad_in.at[block(me), :], grad_s, grad_r
    )
    grad_start()
    grad_in[block(me), :] = grad_out[block(me), :]
    across.wait_send()
    across.wait_recv()
    near = near + squares(1 - my_y)
    for copy in (ss_far, ss_diag):
        copy.wait_send()
        copy.wait_recv()
    beyond = ss_in[0] + ss_in[1]
    beyond = jnp.transpose(jnp.broadcast_to(beyond[0:1, :], (128, both_rows)))[:, 0:1]
    scale = lax.rsqrt((near + beyond) / D + 1e-06)
    for q in range(2):

        def norm(j, carry, q=q):
            normed = (
                xfull[q, 0:both_rows, column(j)].astype(jnp.float32)
                * scale
                * xfull[q, both_rows : both_rows + 1, column(j)].astype(jnp.float32)
            )
            xin[:, column(q * tiles + j)] = normed.astype(jnp.bfloat16)
            return carry

        lax.fori_loop(0, tiles, norm, 0)

    wide = 256
    sends = []
    for k in range(3):
        if k:
            pass_diag(k)
        own_c[k].wait_recv()
        x_core[k].wait_recv()
        z_core[k].wait_recv()
        diag_core[k].wait_recv()

        def project(j, carry, k=k):
            at = pl.ds(pl.multiple_of(j * wide, wide), wide)
            both = jnp.dot(xin[...], wbuf[k, :, at], preferred_element_type=jnp.float32)
            for zs in range(2):
                rows = both[zs * SLOT : (zs + 1) * SLOT]
                part_own[k, zs, :, at] = rows
                part_out[k, zs, :, at] = rows.astype(jnp.bfloat16)
            return carry

        lax.fori_loop(0, qw // wide, project, 0)
        send = remote(
            part_out.at[k, 1 - half], part_in.at[k], p_s.at[k], p_r.at[k], dp=far
        )
        send.start()
        sends.append(send)

    grad_finish()

    def credit(j, carry):
        gsum_ref[:, column(j)] = lax.dot_general(
            want, grad_in[:, column(j)], (((0,), (0,)), ((), ())),
            preferred_element_type=jnp.float32,
        )
        return carry

    lax.fori_loop(0, 2 * tiles, credit, 0)
    for group in (own_x, own_z, own_c, x_on, x_core, z_on, z_core, diag_core):
        for copy in group:
            copy.wait_send()
    key_at = lax.broadcasted_iota(jnp.int32, (SLOT, SLOT), 1)
    query_at = lax.broadcasted_iota(jnp.int32, (SLOT, SLOT), 0)
    length = length_ref[0]
    allowed = (key_at <= query_at) & (key_at < length)
    live = query_at < length

    def whole(k, at):
        total = part_own[k, half, :, at] + part_in[k, :, at].astype(jnp.float32)
        return total.astype(jnp.bfloat16)

    def head_columns(h):
        return pl.ds(pl.multiple_of(h * HD, HD), HD)

    def head_probs(h, carry):
        at = head_columns(h)
        scores = lax.dot_general(
            whole(0, at), whole(1, at), (((1,), (1,)), ((), ())),
            preferred_element_type=jnp.float32,
        ) / math.sqrt(HD)
        scores = jnp.where(allowed, scores, jnp.float32(-1e30))
        powers = jnp.exp(scores - jnp.max(scores, axis=-1, keepdims=True))
        probs_ref[h] = (powers / jnp.sum(powers, axis=-1, keepdims=True)).astype(jnp.bfloat16)
        return carry

    def head_context(h, carry):
        at = head_columns(h)
        context = jnp.dot(probs_ref[h], whole(2, at), preferred_element_type=jnp.float32)
        ctx_ref[:, at] = jnp.where(live, context, jnp.float32(0.0)).astype(jnp.bfloat16)
        return carry

    sends[0].wait_recv()
    sends[1].wait_recv()
    lax.fori_loop(0, qw // HD, head_probs, 0)
    sends[2].wait_recv()
    lax.fori_loop(0, qw // HD, head_context, 0)
    for send in sends:
        send.wait_send()


def local_16(
    session_length, event_owner, event_row, text_rows, image_rows, price, price_dir, norm_gain,
    w_query, w_key, w_value, cotangent,
):
    n = 16
    cap = 16
    tokens = event_row.shape[0]
    width = text_rows.shape[1]
    table = text_rows.shape[0]
    wrows, qw = w_query.shape
    vmem = pl.BlockSpec(memory_space=pltpu.VMEM)
    hbm = pl.BlockSpec(memory_space=pl.ANY)
    dma = pltpu.SemaphoreType.DMA
    bf16 = jnp.bfloat16
    context, gsum = pl.pallas_call(
        exchange_kernel,
        out_shape=(
            jax.ShapeDtypeStruct((tokens, qw), bf16),
            jax.ShapeDtypeStruct((table, width), jnp.float32),
        ),
        in_specs=[pl.BlockSpec(memory_space=pltpu.SMEM)] + [vmem] * 5 + [hbm] * 6,
        out_specs=(vmem, vmem),
        scratch_shapes=[
            pltpu.VMEM((table, width), bf16),
            pltpu.VMEM((table, width), bf16),
            pltpu.VMEM((tokens, width), bf16),
            pltpu.VMEM((n * cap, 128), jnp.int32),
            pltpu.VMEM((qw // HD, tokens, tokens), bf16),
            pltpu.VMEM((n * cap, 128), jnp.int32),
            pltpu.VMEM((2, 8, tokens), jnp.int32),
            pltpu.VMEM((2, table + 16, width // 2), bf16),
            pltpu.VMEM((table + 16, width // 2), bf16),
            pltpu.VMEM((2, 2, 8 * cap, width // 2), bf16),
            pltpu.VMEM((2, n * cap, width // 2), bf16),
            pltpu.VMEM((n * cap, width), bf16),
            pltpu.VMEM((n * cap, width), bf16),
            pltpu.VMEM((16, width), jnp.float32),
            pltpu.VMEM((3, 8 * wrows, qw), bf16),
            pltpu.VMEM((2, 2 * tokens + 16, width // 2), bf16),
            pltpu.VMEM((2 * tokens, width), bf16),
            pltpu.VMEM((8, 2 * tokens), jnp.float32),
            pltpu.VMEM((2, 8, 2 * tokens), jnp.float32),
            pltpu.VMEM((3, 2, tokens, qw), jnp.float32),
            pltpu.VMEM((3, 2, tokens, qw), bf16),
            pltpu.VMEM((3, tokens, qw), bf16),
            dma((6,)), dma((n,)), dma((n,)), dma((n,)), dma((n,)), dma((n,)), dma((n,)),
            dma((24,)), dma((24,)), dma((5,)), dma((5,)), dma((3,)), dma((3,)),
        ],
        compiler_params=pltpu.CompilerParams(
            collective_id=0, has_side_effects=True, vmem_limit_bytes=60 * 1024 * 1024
        ),
    )(
        session_length, event_owner[:, 0], event_row, price, price_dir, norm_gain,
        text_rows, image_rows, cotangent, w_query, w_key, w_value,
    )
    text_grad = gsum * image_rows.astype(jnp.float32)
    image_grad = gsum * text_rows.astype(jnp.float32)
    return (context, text_grad, image_grad)


def solution(mesh):
    fits = mesh.shape["dp"] == 16 and mesh.shape["mp"] == 2
    return jax.shard_map(
        local_16 if fits else local_any,
        mesh=mesh,
        in_specs=(
            P("dp"),
            P("dp", None),
            P("dp"),
            P("dp", "mp"),
            P("dp", "mp"),
            P("dp"),
            P("mp"),
            P("mp"),
            P("dp", "mp"),
            P("dp", "mp"),
            P("dp", "mp"),
            P("dp", "mp"),
        ),
        out_specs=(P("dp", "mp"), P("dp", "mp"), P("dp", "mp")),
        check_vma=False,
    )
```

```python
import math

import jax
import jax.numpy as jnp
from jax import lax
from jax.experimental import pallas as pl
from jax.experimental.pallas import tpu as pltpu
from jax.sharding import PartitionSpec as P

D = 4096
HD = 128
SLOT = 128


def fetch_rows(requests, text_rows, image_rows):
    row_ids = jnp.maximum(requests, 0)
    return (row_ids, text_rows[row_ids], image_rows[row_ids])


def join_rows(row_ids, text_got, image_got, price, price_dir):
    price_got = price[row_ids]
    mixed = text_got.astype(jnp.float32) * image_got.astype(jnp.float32) + price_got[
        ..., None
    ] * price_dir.astype(jnp.float32)
    return mixed.astype(jnp.bfloat16)


def answer(requests, text_rows, image_rows, price, price_dir):
    row_ids, text_got, image_got = fetch_rows(requests, text_rows, image_rows)
    joined_rows = join_rows(row_ids, text_got, image_got, price, price_dir)
    replies = lax.all_to_all(joined_rows, "dp", split_axis=0, concat_axis=0, tiled=True)
    return (replies, row_ids, text_got, image_got)


def credit_rows(row_ids, grad_rows, text_got, image_got, table_rows):
    col_width = grad_rows.shape[-1]
    flat_ids = row_ids.reshape(-1)
    grad_float = grad_rows.astype(jnp.float32)
    text_terms = (grad_float * image_got.astype(jnp.float32)).reshape(-1, col_width)
    image_terms = (grad_float * text_got.astype(jnp.float32)).reshape(-1, col_width)
    text_grad = jax.ops.segment_sum(text_terms, flat_ids, num_segments=table_rows)
    image_grad = jax.ops.segment_sum(image_terms, flat_ids, num_segments=table_rows)
    return (text_grad, image_grad)


def attend(query, keys, values, session_length):
    sessions = session_length.shape[0]
    heads_here = query.shape[1] // HD
    shape4 = (sessions, SLOT, heads_here, HD)
    scores = jnp.einsum(
        "sqhd,skhd->shqk",
        query.reshape(shape4),
        keys.reshape(shape4),
        preferred_element_type=jnp.float32,
    ) / math.sqrt(HD)
    position = jnp.arange(SLOT, dtype=jnp.int32)
    live_mask = position[None, :] < session_length[:, None]
    allowed = (position[None, :] <= position[:, None])[None, None, :, :] & live_mask[
        :, None, None, :
    ]
    scores = jnp.where(allowed, scores, jnp.float32(-1e30))
    row_max = jnp.max(scores, axis=-1, keepdims=True)
    powers = jnp.exp(scores - row_max)
    probs = (powers / jnp.sum(powers, axis=-1, keepdims=True)).astype(jnp.bfloat16)
    context = jnp.einsum(
        "shqk,skhd->sqhd", probs, values.reshape(shape4), preferred_element_type=jnp.float32
    )
    context = jnp.where(live_mask[:, :, None, None], context, jnp.float32(0.0))
    return context.reshape(sessions * SLOT, heads_here * HD).astype(jnp.bfloat16)


def local_any(
    session_length,
    event_owner,
    event_row,
    text_rows,
    image_rows,
    price,
    price_dir,
    norm_gain,
    w_query,
    w_key,
    w_value,
    cotangent,
):
    peers = lax.axis_size("dp")
    tok_count = event_row.shape[0]
    capacity = 2 * tok_count // peers
    col_width = text_rows.shape[1]
    table_rows = text_rows.shape[0]
    owner_ids = event_owner[:, 0]
    member = (owner_ids[:, None] == jnp.arange(peers, dtype=jnp.int32)[None, :]).astype(jnp.int32)
    earlier = jnp.sum((jnp.cumsum(member, axis=0) - member) * member, axis=1)
    slot_ids = owner_ids * capacity + earlier
    requests = (
        jnp.full((peers * capacity,), -1, jnp.int32)
        .at[slot_ids]
        .set(event_row)
        .reshape(peers, capacity)
    )
    grad_buffer = (
        jnp.zeros((peers * capacity, col_width), jnp.bfloat16)
        .at[slot_ids]
        .set(cotangent)
        .reshape(peers, capacity, col_width)
    )
    replies = answer(
        lax.all_to_all(requests, "dp", split_axis=0, concat_axis=0, tiled=True),
        text_rows,
        image_rows,
        price,
        price_dir,
    )[0]
    got_ids, got_grads = (
        lax.all_to_all(requests, "dp", split_axis=0, concat_axis=0, tiled=True),
        lax.all_to_all(grad_buffer, "dp", split_axis=0, concat_axis=0, tiled=True),
    )
    row_ids, text_got, image_got = fetch_rows(got_ids, text_rows, image_rows)
    text_grad, image_grad = credit_rows(row_ids, got_grads, text_got, image_got, table_rows)
    joined_rows = replies.reshape(peers * capacity, col_width)[slot_ids]
    joined_float = joined_rows.astype(jnp.float32)
    square_sums = lax.psum(jnp.sum(joined_float * joined_float, axis=1), "mp")
    scale = lax.rsqrt(square_sums / D + 1e-06)
    normed = (joined_float * scale[:, None] * norm_gain.astype(jnp.float32)[None, :]).astype(
        jnp.bfloat16
    )
    features_all = lax.all_gather(normed, "mp", axis=1, tiled=True)

    def add_rows(weight_rows):
        return jnp.dot(features_all, weight_rows, preferred_element_type=jnp.float32)

    query_sum = add_rows(lax.all_gather(w_query, "dp", axis=0, tiled=True))
    key_sum = add_rows(lax.all_gather(w_key, "dp", axis=0, tiled=True))
    value_sum = add_rows(lax.all_gather(w_value, "dp", axis=0, tiled=True))
    context = attend(
        query_sum.astype(jnp.bfloat16),
        key_sum.astype(jnp.bfloat16),
        value_sum.astype(jnp.bfloat16),
        session_length,
    )
    return (context, text_grad, image_grad)


def flip(index, bit):
    return index + bit - 2 * bit * ((index // bit) % 2)


def exchange_kernel(
    length_ref, owner_ref, row_ref, price_ref, dir_ref, gain_ref, text_hbm, image_hbm, cot_hbm,
    wq_ref, wk_ref, wv_ref,
    ctx_ref, gsum_ref,
    text_ref, image_ref, cot_ref, reqs_ref, probs_ref, ids, slots, tq, tsend, rep_out, rep_in, grad_out, grad_in,
    fvals, wbuf, xfull, xin, ss_out, ss_in, part_own, part_out, part_in,
    load_sem, id_s, id_r, rep_s, rep_r, grad_s, grad_r, w_s, w_r, one_s, one_r, p_s, p_r,
):
    me = lax.axis_index("dp")
    my_y = lax.axis_index("mp")
    n = 16
    cap = 16
    rel = me % 8
    half = me // 8
    far = flip(me, 8)
    wrows = wq_ref.shape[0]
    qw = wq_ref.shape[1]
    quarter = dir_ref.shape[0] // 2
    table = text_ref.shape[0]
    both_rows = 2 * SLOT
    weights_in = (wq_ref, wk_ref, wv_ref)
    table_loads = [
        pltpu.make_async_copy(a, b, load_sem.at[3 + k])
        for k, (a, b) in enumerate(
            ((text_hbm, text_ref), (image_hbm, image_ref), (cot_hbm, cot_ref))
        )
    ]
    w_loads = [
        pltpu.make_async_copy(w, wbuf.at[k, pl.ds(rel * wrows, wrows), :], load_sem.at[k])
        for k, w in enumerate(weights_in)
    ]
    for load in w_loads + table_loads:
        load.start()
    barrier = pltpu.get_barrier_semaphore()

    def greet(i, carry):
        pl.semaphore_signal(
            barrier, inc=1, device_id={"dp": (me + i) % n}, device_id_type=pl.DeviceIdType.MESH
        )
        return carry

    lax.fori_loop(1, n, greet, 0)
    pl.semaphore_signal(
        barrier, inc=1, device_id={"mp": 1 - my_y}, device_id_type=pl.DeviceIdType.MESH
    )
    pl.semaphore_signal(
        barrier, inc=1, device_id={"dp": far, "mp": 1 - my_y},
        device_id_type=pl.DeviceIdType.MESH,
    )

    def lanes(ref, rows):
        return jnp.broadcast_to(ref[...].reshape(1, ref.shape[0]), (rows, ref.shape[0]))

    owner_along = lanes(owner_ref, SLOT)
    before = lax.broadcasted_iota(jnp.int32, (SLOT, SLOT), 0) < lax.broadcasted_iota(
        jnp.int32, (SLOT, SLOT), 1
    )
    same = (jnp.transpose(owner_along) == owner_along) & before
    slot = owner_along[0:1, :] * cap + jnp.sum(same.astype(jnp.int32), axis=0, keepdims=True)
    picked = lax.broadcasted_iota(jnp.int32, (n * cap, SLOT), 0) == slot
    asked = jnp.max(jnp.where(picked, lanes(row_ref, n * cap), -1), axis=1, keepdims=True)
    reqs_ref[...] = jnp.broadcast_to(asked, (n * cap, 128))
    slots[half] = jnp.broadcast_to(slot, (8, SLOT))
    pl.semaphore_wait(barrier, n + 1)

    def remote(src, dst, send, recv, **to):
        return pltpu.make_async_remote_copy(
            src_ref=src, dst_ref=dst, send_sem=send, recv_sem=recv, device_id=to,
            device_id_type=pl.DeviceIdType.MESH,
        )

    def swap(src_of, dst, send, recv):
        def one(i):
            peer = (me + i) % n
            return remote(src_of(peer), dst, send.at[i], recv.at[i], dp=peer)

        def start(i, carry):
            one(i).start()
            return carry

        def finish(i, carry):
            one(i).wait_send()
            one(i).wait_recv()
            return carry

        return (
            lambda: lax.fori_loop(1, n, start, 0),
            lambda: lax.fori_loop(1, n, finish, 0),
        )

    def block(peer):
        return pl.ds(peer * cap, cap)

    id_start, id_finish = swap(
        lambda p: reqs_ref.at[block(p), :], ids.at[block(me), :], id_s, id_r
    )
    id_start()
    slot_out = remote(slots.at[half], slots.at[half], one_s.at[0], one_r.at[0], dp=far)
    slot_out.start()
    ids[block(me), :] = reqs_ref[block(me), :]

    def send_w(k, c, rel_index, bit, low=0, count=wrows):
        part = wbuf.at[k, pl.ds(rel_index * wrows + low, count), :]
        return remote(part, part, w_s.at[8 * k + c], w_r.at[8 * k + c], dp=flip(me, bit))

    zrows = wrows // 4
    own_x = [send_w(k, 0, rel, 2) for k in range(3)]
    own_z = [send_w(k, 1, rel, 4) for k in range(3)]
    own_c = [send_w(k, 2, rel, 1) for k in range(3)]
    x_on = [send_w(k, 3, flip(rel, 2), 4, 0, zrows) for k in range(3)]
    x_core = [send_w(k, 4, flip(rel, 2), 1) for k in range(3)]
    z_on = [send_w(k, 5, flip(rel, 4), 2, zrows, wrows - zrows) for k in range(3)]
    z_core = [send_w(k, 6, flip(rel, 4), 1) for k in range(3)]
    diag_core = [send_w(k, 7, flip(flip(rel, 2), 4), 1) for k in range(3)]

    def pass_on(k):
        own_x[k].wait_recv()
        x_on[k].start()
        x_core[k].start()
        own_z[k].wait_recv()
        z_on[k].start()
        z_core[k].start()

    def pass_diag(k):
        x_on[k].wait_recv()
        z_on[k].wait_recv()
        diag_core[k].start()

    w_loads[0].wait()
    own_x[0].start()
    own_z[0].start()
    own_c[0].start()
    for k in (1, 2):
        w_loads[k].wait()
        own_c[k].start()
    table_loads[0].wait()
    table_loads[1].wait()
    tile = 512
    tiles = quarter // tile
    price = jnp.transpose(lanes(price_ref, 128))[:, 0:1]
    dir_row = dir_ref[...].astype(jnp.float32).reshape(1, 2 * quarter)
    gain_row = gain_ref[...].astype(jnp.float32).reshape(1, 2 * quarter)
    fvals[0:1, :] = dir_row
    fvals[8:9, :] = gain_row

    def join(start, j):
        src = pl.ds(pl.multiple_of(start + j * tile, tile), tile)
        mixed = text_ref[:, src].astype(jnp.float32) * image_ref[:, src].astype(
            jnp.float32
        ) + price * fvals[0:1, src]
        gain = jnp.broadcast_to(fvals[8:9, src], (16, tile))
        return mixed.astype(jnp.bfloat16), gain.astype(jnp.bfloat16)

    def column(j):
        return pl.ds(pl.multiple_of(j * tile, tile), tile)

    def join_out(j, carry):
        rows, gain = join((1 - my_y) * quarter, j)
        tsend[0:table, column(j)] = rows
        tsend[table : table + 16, column(j)] = gain
        return carry

    def join_own(j, carry):
        rows, gain = join(my_y * quarter, j)
        tq[my_y, 0:table, column(j)] = rows
        tq[my_y, table : table + 16, column(j)] = gain
        return carry

    lax.fori_loop(0, tiles, join_out, 0)
    table_out = remote(tsend, tq.at[my_y], one_s.at[1], one_r.at[1], mp=1 - my_y)
    table_out.start()
    lax.fori_loop(0, tiles, join_own, 0)

    def pick_of(slot):
        return (
            lax.broadcasted_iota(jnp.int32, (n * cap, SLOT), 0) == slot
        ).astype(jnp.float32).astype(jnp.bfloat16)

    id_finish()
    got = ids[...]
    lane = lax.broadcasted_iota(jnp.int32, got.shape, 1)
    want = jnp.concatenate(
        [(got == lane + 128 * k).astype(jnp.float32) for k in range(table // 128)], axis=1
    ).astype(jnp.bfloat16)
    table_out.wait_send()
    table_out.wait_recv()
    for m in range(2):

        def reply(j, carry, m=m):
            rows = jnp.dot(
                want, tq[m, 0:table, column(j)], preferred_element_type=jnp.float32
            ).astype(jnp.bfloat16)
            rep_out[m, 0, :, column(j)] = rows[: 8 * cap]
            rep_out[m, 1, :, column(j)] = rows[8 * cap :]
            return carry

        lax.fori_loop(0, tiles, reply, 0)
    rep_start, rep_finish = swap(
        lambda p: rep_out.at[p // 8, :, block(p % 8), :], rep_in.at[:, block(me), :],
        rep_s, rep_r,
    )
    rep_start()
    own_x[1].start()
    rep_in[:, block(me), :] = rep_out[half, :, block(rel), :]
    table_loads[2].wait()
    pick = pick_of(slots[half, 0:1, :])

    def pack_grads(j, carry):
        grad_out[:, column(j)] = jnp.dot(
            pick, cot_ref[:, column(j)], preferred_element_type=jnp.float32
        ).astype(jnp.bfloat16)
        return carry

    lax.fori_loop(0, 2 * tiles, pack_grads, 0)
    pass_on(0)
    slot_out.wait_send()
    slot_out.wait_recv()
    rep_finish()
    own_z[1].start()
    own_x[2].start()

    for zs in range(2):
        chosen = pick_of(slots[zs, 0:1, :])

        def unpack(j, carry, zs=zs, chosen=chosen):
            xfull[my_y, zs * SLOT : (zs + 1) * SLOT, column(j)] = lax.dot_general(
                chosen, rep_in[zs, :, column(j)], (((0,), (0,)), ((), ())),
                preferred_element_type=jnp.float32,
            ).astype(jnp.bfloat16)
            return carry

        lax.fori_loop(0, tiles, unpack, 0)
    xfull[my_y, both_rows : both_rows + 16, :] = tq[half, table : table + 16, :]
    across = remote(xfull.at[my_y], xfull.at[my_y], one_s.at[2], one_r.at[2], mp=1 - my_y)
    across.start()

    def squares(q):
        def add(j, total):
            a = xfull[q, 0:both_rows, column(j)].astype(jnp.float32)
            return total + jnp.sum(a * a, axis=1, keepdims=True)

        return lax.fori_loop(0, tiles, add, jnp.zeros((both_rows, 1), jnp.float32))

    near = squares(my_y)
    ss_out[...] = jnp.transpose(jnp.broadcast_to(near, (both_rows, 128)))[0:8, :]
    ss_far = remote(ss_out, ss_in.at[0], one_s.at[3], one_r.at[3], dp=far)
    ss_far.start()
    ss_diag = remote(ss_out, ss_in.at[1], one_s.at[4], one_r.at[4], dp=far, mp=1 - my_y)
    ss_diag.start()
    pass_diag(0)
    grad_start, grad_finish = swap(
        lambda p: grad_out.at[block(p), :], grad_in.at[block(me), :], grad_s, grad_r
    )
    across.wait_send()
    across.wait_recv()
    own_z[2].start()
    near = near + squares(1 - my_y)
    for copy in (ss_far, ss_diag):
        copy.wait_send()
        copy.wait_recv()
    beyond = ss_in[0] + ss_in[1]
    beyond = jnp.transpose(jnp.broadcast_to(beyond[0:1, :], (128, both_rows)))[:, 0:1]
    scale = lax.rsqrt((near + beyond) / D + 1e-06)
    for q in range(2):

        def norm(j, carry, q=q):
            normed = (
                xfull[q, 0:both_rows, column(j)].astype(jnp.float32)
                * scale
                * xfull[q, both_rows : both_rows + 1, column(j)].astype(jnp.float32)
            )
            xin[:, column(q * tiles + j)] = normed.astype(jnp.bfloat16)
            return carry

        lax.fori_loop(0, tiles, norm, 0)

    wide = 256
    sends = []
    for k in range(3):
        if k:
            pass_on(k)
            if k == 1:
                grad_start()
                grad_in[block(me), :] = grad_out[block(me), :]
            pass_diag(k)
        own_c[k].wait_recv()
        x_core[k].wait_recv()
        z_core[k].wait_recv()
        diag_core[k].wait_recv()

        def project(j, carry, k=k):
            at = pl.ds(pl.multiple_of(j * wide, wide), wide)
            both = jnp.dot(xin[...], wbuf[k, :, at], preferred_element_type=jnp.float32)
            for zs in range(2):
                rows = both[zs * SLOT : (zs + 1) * SLOT]
                part_own[k, zs, :, at] = rows
                part_out[k, zs, :, at] = rows.astype(jnp.bfloat16)
            return carry

        lax.fori_loop(0, qw // wide, project, 0)
        send = remote(
            part_out.at[k, 1 - half], part_in.at[k], p_s.at[k], p_r.at[k], dp=far
        )
        send.start()
        sends.append(send)

    grad_finish()

    def credit(j, carry):
        gsum_ref[:, column(j)] = lax.dot_general(
            want, grad_in[:, column(j)], (((0,), (0,)), ((), ())),
            preferred_element_type=jnp.float32,
        )
        return carry

    lax.fori_loop(0, 2 * tiles, credit, 0)
    for group in (own_x, own_z, own_c, x_on, x_core, z_on, z_core, diag_core):
        for copy in group:
            copy.wait_send()
    key_at = lax.broadcasted_iota(jnp.int32, (SLOT, SLOT), 1)
    query_at = lax.broadcasted_iota(jnp.int32, (SLOT, SLOT), 0)
    length = length_ref[0]
    allowed = (key_at <= query_at) & (key_at < length)
    live = query_at < length

    def whole(k, at):
        total = part_own[k, half, :, at] + part_in[k, :, at].astype(jnp.float32)
        return total.astype(jnp.bfloat16)

    def head_columns(h):
        return pl.ds(pl.multiple_of(h * HD, HD), HD)

    def head_probs(h, carry):
        at = head_columns(h)
        scores = lax.dot_general(
            whole(0, at), whole(1, at), (((1,), (1,)), ((), ())),
            preferred_element_type=jnp.float32,
        ) / math.sqrt(HD)
        scores = jnp.where(allowed, scores, jnp.float32(-1e30))
        powers = jnp.exp(scores - jnp.max(scores, axis=-1, keepdims=True))
        probs_ref[h] = (powers / jnp.sum(powers, axis=-1, keepdims=True)).astype(jnp.bfloat16)
        return carry

    def head_context(h, carry):
        at = head_columns(h)
        context = jnp.dot(probs_ref[h], whole(2, at), preferred_element_type=jnp.float32)
        ctx_ref[:, at] = jnp.where(live, context, jnp.float32(0.0)).astype(jnp.bfloat16)
        return carry

    sends[0].wait_recv()
    sends[1].wait_recv()
    lax.fori_loop(0, qw // HD, head_probs, 0)
    sends[2].wait_recv()
    lax.fori_loop(0, qw // HD, head_context, 0)
    for send in sends:
        send.wait_send()


def local_16(
    session_length, event_owner, event_row, text_rows, image_rows, price, price_dir, norm_gain,
    w_query, w_key, w_value, cotangent,
):
    n = 16
    cap = 16
    tokens = event_row.shape[0]
    width = text_rows.shape[1]
    table = text_rows.shape[0]
    wrows, qw = w_query.shape
    vmem = pl.BlockSpec(memory_space=pltpu.VMEM)
    hbm = pl.BlockSpec(memory_space=pl.ANY)
    dma = pltpu.SemaphoreType.DMA
    bf16 = jnp.bfloat16
    context, gsum = pl.pallas_call(
        exchange_kernel,
        out_shape=(
            jax.ShapeDtypeStruct((tokens, qw), bf16),
            jax.ShapeDtypeStruct((table, width), jnp.float32),
        ),
        in_specs=[pl.BlockSpec(memory_space=pltpu.SMEM)] + [vmem] * 5 + [hbm] * 6,
        out_specs=(vmem, vmem),
        scratch_shapes=[
            pltpu.VMEM((table, width), bf16),
            pltpu.VMEM((table, width), bf16),
            pltpu.VMEM((tokens, width), bf16),
            pltpu.VMEM((n * cap, 128), jnp.int32),
            pltpu.VMEM((qw // HD, tokens, tokens), bf16),
            pltpu.VMEM((n * cap, 128), jnp.int32),
            pltpu.VMEM((2, 8, tokens), jnp.int32),
            pltpu.VMEM((2, table + 16, width // 2), bf16),
            pltpu.VMEM((table + 16, width // 2), bf16),
            pltpu.VMEM((2, 2, 8 * cap, width // 2), bf16),
            pltpu.VMEM((2, n * cap, width // 2), bf16),
            pltpu.VMEM((n * cap, width), bf16),
            pltpu.VMEM((n * cap, width), bf16),
            pltpu.VMEM((16, width), jnp.float32),
            pltpu.VMEM((3, 8 * wrows, qw), bf16),
            pltpu.VMEM((2, 2 * tokens + 16, width // 2), bf16),
            pltpu.VMEM((2 * tokens, width), bf16),
            pltpu.VMEM((8, 2 * tokens), jnp.float32),
            pltpu.VMEM((2, 8, 2 * tokens), jnp.float32),
            pltpu.VMEM((3, 2, tokens, qw), jnp.float32),
            pltpu.VMEM((3, 2, tokens, qw), bf16),
            pltpu.VMEM((3, tokens, qw), bf16),
            dma((6,)), dma((n,)), dma((n,)), dma((n,)), dma((n,)), dma((n,)), dma((n,)),
            dma((24,)), dma((24,)), dma((5,)), dma((5,)), dma((3,)), dma((3,)),
        ],
        compiler_params=pltpu.CompilerParams(
            collective_id=0, has_side_effects=True, vmem_limit_bytes=60 * 1024 * 1024
        ),
    )(
        session_length, event_owner[:, 0], event_row, price, price_dir, norm_gain,
        text_rows, image_rows, cotangent, w_query, w_key, w_value,
    )
    text_grad = gsum * image_rows.astype(jnp.float32)
    image_grad = gsum * text_rows.astype(jnp.float32)
    return (context, text_grad, image_grad)


def solution(mesh):
    fits = mesh.shape["dp"] == 16 and mesh.shape["mp"] == 2
    return jax.shard_map(
        local_16 if fits else local_any,
        mesh=mesh,
        in_specs=(
            P("dp"),
            P("dp", None),
            P("dp"),
            P("dp", "mp"),
            P("dp", "mp"),
            P("dp"),
            P("mp"),
            P("mp"),
            P("dp", "mp"),
            P("dp", "mp"),
            P("dp", "mp"),
            P("dp", "mp"),
        ),
        out_specs=(P("dp", "mp"), P("dp", "mp"), P("dp", "mp")),
        check_vma=False,
    )
```

```python
import math

import jax
import jax.numpy as jnp
from jax import lax
from jax.experimental import pallas as pl
from jax.experimental.pallas import tpu as pltpu
from jax.sharding import PartitionSpec as P

D = 4096
HD = 128
SLOT = 128


def fetch_rows(requests, text_rows, image_rows):
    row_ids = jnp.maximum(requests, 0)
    return (row_ids, text_rows[row_ids], image_rows[row_ids])


def join_rows(row_ids, text_got, image_got, price, price_dir):
    price_got = price[row_ids]
    mixed = text_got.astype(jnp.float32) * image_got.astype(jnp.float32) + price_got[
        ..., None
    ] * price_dir.astype(jnp.float32)
    return mixed.astype(jnp.bfloat16)


def answer(requests, text_rows, image_rows, price, price_dir):
    row_ids, text_got, image_got = fetch_rows(requests, text_rows, image_rows)
    joined_rows = join_rows(row_ids, text_got, image_got, price, price_dir)
    replies = lax.all_to_all(joined_rows, "dp", split_axis=0, concat_axis=0, tiled=True)
    return (replies, row_ids, text_got, image_got)


def credit_rows(row_ids, grad_rows, text_got, image_got, table_rows):
    col_width = grad_rows.shape[-1]
    flat_ids = row_ids.reshape(-1)
    grad_float = grad_rows.astype(jnp.float32)
    text_terms = (grad_float * image_got.astype(jnp.float32)).reshape(-1, col_width)
    image_terms = (grad_float * text_got.astype(jnp.float32)).reshape(-1, col_width)
    text_grad = jax.ops.segment_sum(text_terms, flat_ids, num_segments=table_rows)
    image_grad = jax.ops.segment_sum(image_terms, flat_ids, num_segments=table_rows)
    return (text_grad, image_grad)


def attend(query, keys, values, session_length):
    sessions = session_length.shape[0]
    heads_here = query.shape[1] // HD
    shape4 = (sessions, SLOT, heads_here, HD)
    scores = jnp.einsum(
        "sqhd,skhd->shqk",
        query.reshape(shape4),
        keys.reshape(shape4),
        preferred_element_type=jnp.float32,
    ) / math.sqrt(HD)
    position = jnp.arange(SLOT, dtype=jnp.int32)
    live_mask = position[None, :] < session_length[:, None]
    allowed = (position[None, :] <= position[:, None])[None, None, :, :] & live_mask[
        :, None, None, :
    ]
    scores = jnp.where(allowed, scores, jnp.float32(-1e30))
    row_max = jnp.max(scores, axis=-1, keepdims=True)
    powers = jnp.exp(scores - row_max)
    probs = (powers / jnp.sum(powers, axis=-1, keepdims=True)).astype(jnp.bfloat16)
    context = jnp.einsum(
        "shqk,skhd->sqhd", probs, values.reshape(shape4), preferred_element_type=jnp.float32
    )
    context = jnp.where(live_mask[:, :, None, None], context, jnp.float32(0.0))
    return context.reshape(sessions * SLOT, heads_here * HD).astype(jnp.bfloat16)


def local_any(
    session_length,
    event_owner,
    event_row,
    text_rows,
    image_rows,
    price,
    price_dir,
    norm_gain,
    w_query,
    w_key,
    w_value,
    cotangent,
):
    peers = lax.axis_size("dp")
    tok_count = event_row.shape[0]
    capacity = 2 * tok_count // peers
    col_width = text_rows.shape[1]
    table_rows = text_rows.shape[0]
    owner_ids = event_owner[:, 0]
    member = (owner_ids[:, None] == jnp.arange(peers, dtype=jnp.int32)[None, :]).astype(jnp.int32)
    earlier = jnp.sum((jnp.cumsum(member, axis=0) - member) * member, axis=1)
    slot_ids = owner_ids * capacity + earlier
    requests = (
        jnp.full((peers * capacity,), -1, jnp.int32)
        .at[slot_ids]
        .set(event_row)
        .reshape(peers, capacity)
    )
    grad_buffer = (
        jnp.zeros((peers * capacity, col_width), jnp.bfloat16)
        .at[slot_ids]
        .set(cotangent)
        .reshape(peers, capacity, col_width)
    )
    replies = answer(
        lax.all_to_all(requests, "dp", split_axis=0, concat_axis=0, tiled=True),
        text_rows,
        image_rows,
        price,
        price_dir,
    )[0]
    got_ids, got_grads = (
        lax.all_to_all(requests, "dp", split_axis=0, concat_axis=0, tiled=True),
        lax.all_to_all(grad_buffer, "dp", split_axis=0, concat_axis=0, tiled=True),
    )
    row_ids, text_got, image_got = fetch_rows(got_ids, text_rows, image_rows)
    text_grad, image_grad = credit_rows(row_ids, got_grads, text_got, image_got, table_rows)
    joined_rows = replies.reshape(peers * capacity, col_width)[slot_ids]
    joined_float = joined_rows.astype(jnp.float32)
    square_sums = lax.psum(jnp.sum(joined_float * joined_float, axis=1), "mp")
    scale = lax.rsqrt(square_sums / D + 1e-06)
    normed = (joined_float * scale[:, None] * norm_gain.astype(jnp.float32)[None, :]).astype(
        jnp.bfloat16
    )
    features_all = lax.all_gather(normed, "mp", axis=1, tiled=True)

    def add_rows(weight_rows):
        return jnp.dot(features_all, weight_rows, preferred_element_type=jnp.float32)

    query_sum = add_rows(lax.all_gather(w_query, "dp", axis=0, tiled=True))
    key_sum = add_rows(lax.all_gather(w_key, "dp", axis=0, tiled=True))
    value_sum = add_rows(lax.all_gather(w_value, "dp", axis=0, tiled=True))
    context = attend(
        query_sum.astype(jnp.bfloat16),
        key_sum.astype(jnp.bfloat16),
        value_sum.astype(jnp.bfloat16),
        session_length,
    )
    return (context, text_grad, image_grad)


def flip(index, bit):
    return index + bit - 2 * bit * ((index // bit) % 2)


def exchange_kernel(
    length_ref, owner_ref, row_ref, price_ref, dir_ref, gain_ref, text_hbm, image_hbm, cot_hbm,
    wq_ref, wk_ref, wv_ref,
    ctx_ref, gsum_ref,
    text_ref, image_ref, cot_ref, reqs_ref, probs_ref, ids, slots, tq, tsend, rep_out, rep_in, grad_out, grad_in,
    fvals, wbuf, xfull, xin, ss_out, ss_in, part_own, part_out, part_in,
    load_sem, id_s, id_r, rep_s, rep_r, grad_s, grad_r, w_s, w_r, one_s, one_r, p_s, p_r,
):
    me = lax.axis_index("dp")
    my_y = lax.axis_index("mp")
    n = 16
    cap = 16
    rel = me % 8
    half = me // 8
    far = flip(me, 8)
    wrows = wq_ref.shape[0]
    qw = wq_ref.shape[1]
    quarter = dir_ref.shape[0] // 2
    table = text_ref.shape[0]
    both_rows = 2 * SLOT
    weights_in = (wq_ref, wk_ref, wv_ref)
    table_loads = [
        pltpu.make_async_copy(a, b, load_sem.at[3 + k])
        for k, (a, b) in enumerate(
            ((text_hbm, text_ref), (image_hbm, image_ref), (cot_hbm, cot_ref))
        )
    ]
    w_loads = [
        pltpu.make_async_copy(w, wbuf.at[k, pl.ds(rel * wrows, wrows), :], load_sem.at[k])
        for k, w in enumerate(weights_in)
    ]
    for load in w_loads + table_loads:
        load.start()
    barrier = pltpu.get_barrier_semaphore()

    def greet(i, carry):
        pl.semaphore_signal(
            barrier, inc=1, device_id={"dp": (me + i) % n}, device_id_type=pl.DeviceIdType.MESH
        )
        return carry

    lax.fori_loop(1, n, greet, 0)
    pl.semaphore_signal(
        barrier, inc=1, device_id={"mp": 1 - my_y}, device_id_type=pl.DeviceIdType.MESH
    )
    pl.semaphore_signal(
        barrier, inc=1, device_id={"dp": far, "mp": 1 - my_y},
        device_id_type=pl.DeviceIdType.MESH,
    )

    def lanes(ref, rows):
        return jnp.broadcast_to(ref[...].reshape(1, ref.shape[0]), (rows, ref.shape[0]))

    owner_along = lanes(owner_ref, SLOT)
    before = lax.broadcasted_iota(jnp.int32, (SLOT, SLOT), 0) < lax.broadcasted_iota(
        jnp.int32, (SLOT, SLOT), 1
    )
    same = (jnp.transpose(owner_along) == owner_along) & before
    slot = owner_along[0:1, :] * cap + jnp.sum(same.astype(jnp.int32), axis=0, keepdims=True)
    picked = lax.broadcasted_iota(jnp.int32, (n * cap, SLOT), 0) == slot
    asked = jnp.max(jnp.where(picked, lanes(row_ref, n * cap), -1), axis=1, keepdims=True)
    reqs_ref[...] = jnp.broadcast_to(asked, (n * cap, 128))
    slots[half] = jnp.broadcast_to(slot, (8, SLOT))
    pl.semaphore_wait(barrier, n + 1)

    def remote(src, dst, send, recv, **to):
        return pltpu.make_async_remote_copy(
            src_ref=src, dst_ref=dst, send_sem=send, recv_sem=recv, device_id=to,
            device_id_type=pl.DeviceIdType.MESH,
        )

    def swap(src_of, dst, send, recv, base=0):
        def one(i):
            peer = (me + i) % n
            return remote(src_of(peer), dst, send.at[base + i], recv.at[base + i], dp=peer)

        def start(i, carry):
            one(i).start()
            return carry

        def finish(i, carry):
            one(i).wait_send()
            one(i).wait_recv()
            return carry

        return (
            lambda: lax.fori_loop(1, n, start, 0),
            lambda: lax.fori_loop(1, n, finish, 0),
        )

    def block(peer):
        return pl.ds(peer * cap, cap)

    id_start, id_finish = swap(
        lambda p: reqs_ref.at[block(p), :], ids.at[block(me), :], id_s, id_r
    )
    id_start()
    slot_out = remote(slots.at[half], slots.at[half], one_s.at[0], one_r.at[0], dp=far)
    slot_out.start()
    ids[block(me), :] = reqs_ref[block(me), :]

    def send_w(k, c, rel_index, bit, low=0, count=wrows):
        part = wbuf.at[k, pl.ds(rel_index * wrows + low, count), :]
        return remote(part, part, w_s.at[8 * k + c], w_r.at[8 * k + c], dp=flip(me, bit))

    zrows = wrows // 4
    own_x = [send_w(k, 0, rel, 2) for k in range(3)]
    own_z = [send_w(k, 1, rel, 4) for k in range(3)]
    own_c = [send_w(k, 2, rel, 1) for k in range(3)]
    x_on = [send_w(k, 3, flip(rel, 2), 4, 0, zrows) for k in range(3)]
    x_core = [send_w(k, 4, flip(rel, 2), 1) for k in range(3)]
    z_on = [send_w(k, 5, flip(rel, 4), 2, zrows, wrows - zrows) for k in range(3)]
    z_core = [send_w(k, 6, flip(rel, 4), 1) for k in range(3)]
    diag_core = [send_w(k, 7, flip(flip(rel, 2), 4), 1) for k in range(3)]

    def pass_on(k):
        own_x[k].wait_recv()
        x_on[k].start()
        x_core[k].start()
        own_z[k].wait_recv()
        z_on[k].start()
        z_core[k].start()

    def pass_diag(k):
        x_on[k].wait_recv()
        z_on[k].wait_recv()
        diag_core[k].start()

    w_loads[0].wait()
    own_x[0].start()
    own_z[0].start()
    own_c[0].start()
    for k in (1, 2):
        w_loads[k].wait()
        own_c[k].start()
    table_loads[0].wait()
    table_loads[1].wait()
    tile = 512
    tiles = quarter // tile
    price = jnp.transpose(lanes(price_ref, 128))[:, 0:1]
    dir_row = dir_ref[...].astype(jnp.float32).reshape(1, 2 * quarter)
    gain_row = gain_ref[...].astype(jnp.float32).reshape(1, 2 * quarter)
    fvals[0:1, :] = dir_row
    fvals[8:9, :] = gain_row

    def join(start, j):
        src = pl.ds(pl.multiple_of(start + j * tile, tile), tile)
        mixed = text_ref[:, src].astype(jnp.float32) * image_ref[:, src].astype(
            jnp.float32
        ) + price * fvals[0:1, src]
        gain = jnp.broadcast_to(fvals[8:9, src], (16, tile))
        return mixed.astype(jnp.bfloat16), gain.astype(jnp.bfloat16)

    def column(j):
        return pl.ds(pl.multiple_of(j * tile, tile), tile)

    def join_out(j, carry):
        rows, gain = join((1 - my_y) * quarter, j)
        tsend[0:table, column(j)] = rows
        tsend[table : table + 16, column(j)] = gain
        return carry

    def join_own(j, carry):
        rows, gain = join(my_y * quarter, j)
        tq[my_y, 0:table, column(j)] = rows
        tq[my_y, table : table + 16, column(j)] = gain
        return carry

    def piece(c):
        return pl.ds(c * tile, tile)

    table_out = [
        remote(
            tsend.at[:, piece(c)], tq.at[my_y, :, piece(c)], one_s.at[5 + c], one_r.at[5 + c],
            mp=1 - my_y,
        )
        for c in range(tiles)
    ]
    for c in range(tiles):
        join_out(c, 0)
        table_out[c].start()
    lax.fori_loop(0, tiles, join_own, 0)

    def pick_of(slot):
        return (
            lax.broadcasted_iota(jnp.int32, (n * cap, SLOT), 0) == slot
        ).astype(jnp.float32).astype(jnp.bfloat16)

    id_finish()
    got = ids[...]
    lane = lax.broadcasted_iota(jnp.int32, got.shape, 1)
    want = jnp.concatenate(
        [(got == lane + 128 * k).astype(jnp.float32) for k in range(table // 128)], axis=1
    ).astype(jnp.bfloat16)
    replies = [
        swap(
            lambda p, c=c: rep_out.at[p // 8, :, block(p % 8), piece(c)],
            rep_in.at[:, block(me), piece(c)],
            rep_s, rep_r, c * n,
        )
        for c in range(tiles)
    ]
    for c in range(tiles):
        table_out[c].wait_send()
        table_out[c].wait_recv()
        for m in range(2):
            rows = jnp.dot(
                want, tq[m, 0:table, piece(c)], preferred_element_type=jnp.float32
            ).astype(jnp.bfloat16)
            rep_out[m, 0, :, piece(c)] = rows[: 8 * cap]
            rep_out[m, 1, :, piece(c)] = rows[8 * cap :]
        replies[c][0]()
    own_x[1].start()
    rep_in[:, block(me), :] = rep_out[half, :, block(rel), :]
    table_loads[2].wait()
    pick = pick_of(slots[half, 0:1, :])

    def pack_grads(j, carry):
        grad_out[:, column(j)] = jnp.dot(
            pick, cot_ref[:, column(j)], preferred_element_type=jnp.float32
        ).astype(jnp.bfloat16)
        return carry

    lax.fori_loop(0, 2 * tiles, pack_grads, 0)
    pass_on(0)
    slot_out.wait_send()
    slot_out.wait_recv()
    chosen = [pick_of(slots[zs, 0:1, :]) for zs in range(2)]
    across = []
    for c in range(tiles):
        replies[c][1]()
        if c == tiles - 1:
            own_z[1].start()
            own_x[2].start()
        for zs in range(2):
            xfull[my_y, zs * SLOT : (zs + 1) * SLOT, piece(c)] = lax.dot_general(
                chosen[zs], rep_in[zs, :, piece(c)], (((0,), (0,)), ((), ())),
                preferred_element_type=jnp.float32,
            ).astype(jnp.bfloat16)
        xfull[my_y, both_rows : both_rows + 16, piece(c)] = tq[
            half, table : table + 16, piece(c)
        ]
        part = xfull.at[my_y, :, piece(c)]
        across.append(remote(part, part, one_s.at[1 + c], one_r.at[1 + c], mp=1 - my_y))
        across[c].start()
    grad_start, grad_finish = swap(
        lambda p: grad_out.at[block(p), :], grad_in.at[block(me), :], grad_s, grad_r
    )
    grad_start()
    own_z[2].start()
    grad_in[block(me), :] = grad_out[block(me), :]

    def squares(q):
        def add(j, total):
            a = xfull[q, 0:both_rows, column(j)].astype(jnp.float32)
            return total + jnp.sum(a * a, axis=1, keepdims=True)

        return lax.fori_loop(0, tiles, add, jnp.zeros((both_rows, 1), jnp.float32))

    near = squares(my_y)
    ss_out[...] = jnp.transpose(jnp.broadcast_to(near, (both_rows, 128)))[0:8, :]
    ss_far = remote(ss_out, ss_in.at[0], one_s.at[3], one_r.at[3], dp=far)
    ss_far.start()
    ss_diag = remote(ss_out, ss_in.at[1], one_s.at[4], one_r.at[4], dp=far, mp=1 - my_y)
    ss_diag.start()
    pass_diag(0)
    for copy in across:
        copy.wait_send()
        copy.wait_recv()
    near = near + squares(1 - my_y)
    for copy in (ss_far, ss_diag):
        copy.wait_send()
        copy.wait_recv()
    beyond = ss_in[0] + ss_in[1]
    beyond = jnp.transpose(jnp.broadcast_to(beyond[0:1, :], (128, both_rows)))[:, 0:1]
    scale = lax.rsqrt((near + beyond) / D + 1e-06)
    for q in range(2):

        def norm(j, carry, q=q):
            normed = (
                xfull[q, 0:both_rows, column(j)].astype(jnp.float32)
                * scale
                * xfull[q, both_rows : both_rows + 1, column(j)].astype(jnp.float32)
            )
            xin[:, column(q * tiles + j)] = normed.astype(jnp.bfloat16)
            return carry

        lax.fori_loop(0, tiles, norm, 0)

    wide = 256
    sends = []
    for k in range(3):
        if k:
            pass_on(k)
            pass_diag(k)
        own_c[k].wait_recv()
        x_core[k].wait_recv()
        z_core[k].wait_recv()
        diag_core[k].wait_recv()

        def project(j, carry, k=k):
            at = pl.ds(pl.multiple_of(j * wide, wide), wide)
            both = jnp.dot(xin[...], wbuf[k, :, at], preferred_element_type=jnp.float32)
            for zs in range(2):
                rows = both[zs * SLOT : (zs + 1) * SLOT]
                part_own[k, zs, :, at] = rows
                part_out[k, zs, :, at] = rows.astype(jnp.bfloat16)
            return carry

        steps = qw // wide // 2
        for h in range(2):
            lax.fori_loop(h * steps, (h + 1) * steps, project, 0)
            cols = pl.ds(h * (qw // 2), qw // 2)
            send = remote(
                part_out.at[k, 1 - half, :, cols], part_in.at[k, :, cols],
                p_s.at[2 * k + h], p_r.at[2 * k + h], dp=far,
            )
            send.start()
            sends.append(send)

    key_at = lax.broadcasted_iota(jnp.int32, (SLOT, SLOT), 1)
    query_at = lax.broadcasted_iota(jnp.int32, (SLOT, SLOT), 0)
    length = length_ref[0]
    allowed = (key_at <= query_at) & (key_at < length)
    live = query_at < length

    def whole(k, at):
        total = part_own[k, half, :, at] + part_in[k, :, at].astype(jnp.float32)
        return total.astype(jnp.bfloat16)

    def head_columns(h):
        return pl.ds(pl.multiple_of(h * HD, HD), HD)

    def head_probs(h, carry):
        at = head_columns(h)
        scores = lax.dot_general(
            whole(0, at), whole(1, at), (((1,), (1,)), ((), ())),
            preferred_element_type=jnp.float32,
        ) / math.sqrt(HD)
        scores = jnp.where(allowed, scores, jnp.float32(-1e30))
        powers = jnp.exp(scores - jnp.max(scores, axis=-1, keepdims=True))
        probs_ref[h] = (powers / jnp.sum(powers, axis=-1, keepdims=True)).astype(jnp.bfloat16)
        return carry

    def head_context(h, carry):
        at = head_columns(h)
        context = jnp.dot(probs_ref[h], whole(2, at), preferred_element_type=jnp.float32)
        ctx_ref[:, at] = jnp.where(live, context, jnp.float32(0.0)).astype(jnp.bfloat16)
        return carry

    for send in sends[:4]:
        send.wait_recv()
    lax.fori_loop(0, qw // HD, head_probs, 0)
    grad_finish()

    def credit(j, carry):
        gsum_ref[:, column(j)] = lax.dot_general(
            want, grad_in[:, column(j)], (((0,), (0,)), ((), ())),
            preferred_element_type=jnp.float32,
        )
        return carry

    lax.fori_loop(0, 2 * tiles, credit, 0)
    for group in (own_x, own_z, own_c, x_on, x_core, z_on, z_core, diag_core):
        for copy in group:
            copy.wait_send()
    half_heads = qw // HD // 2
    for h in range(2):
        sends[4 + h].wait_recv()
        lax.fori_loop(h * half_heads, (h + 1) * half_heads, head_context, 0)
    for send in sends:
        send.wait_send()


def local_16(
    session_length, event_owner, event_row, text_rows, image_rows, price, price_dir, norm_gain,
    w_query, w_key, w_value, cotangent,
):
    n = 16
    cap = 16
    tokens = event_row.shape[0]
    width = text_rows.shape[1]
    table = text_rows.shape[0]
    wrows, qw = w_query.shape
    vmem = pl.BlockSpec(memory_space=pltpu.VMEM)
    hbm = pl.BlockSpec(memory_space=pl.ANY)
    dma = pltpu.SemaphoreType.DMA
    bf16 = jnp.bfloat16
    context, gsum = pl.pallas_call(
        exchange_kernel,
        out_shape=(
            jax.ShapeDtypeStruct((tokens, qw), bf16),
            jax.ShapeDtypeStruct((table, width), jnp.float32),
        ),
        in_specs=[pl.BlockSpec(memory_space=pltpu.SMEM)] + [vmem] * 5 + [hbm] * 6,
        out_specs=(vmem, vmem),
        scratch_shapes=[
            pltpu.VMEM((table, width), bf16),
            pltpu.VMEM((table, width), bf16),
            pltpu.VMEM((tokens, width), bf16),
            pltpu.VMEM((n * cap, 128), jnp.int32),
            pltpu.VMEM((qw // HD, tokens, tokens), bf16),
            pltpu.VMEM((n * cap, 128), jnp.int32),
            pltpu.VMEM((2, 8, tokens), jnp.int32),
            pltpu.VMEM((2, table + 16, width // 2), bf16),
            pltpu.VMEM((table + 16, width // 2), bf16),
            pltpu.VMEM((2, 2, 8 * cap, width // 2), bf16),
            pltpu.VMEM((2, n * cap, width // 2), bf16),
            pltpu.VMEM((n * cap, width), bf16),
            pltpu.VMEM((n * cap, width), bf16),
            pltpu.VMEM((16, width), jnp.float32),
            pltpu.VMEM((3, 8 * wrows, qw), bf16),
            pltpu.VMEM((2, 2 * tokens + 16, width // 2), bf16),
            pltpu.VMEM((2 * tokens, width), bf16),
            pltpu.VMEM((8, 2 * tokens), jnp.float32),
            pltpu.VMEM((2, 8, 2 * tokens), jnp.float32),
            pltpu.VMEM((3, 2, tokens, qw), jnp.float32),
            pltpu.VMEM((3, 2, tokens, qw), bf16),
            pltpu.VMEM((3, tokens, qw), bf16),
            dma((6,)), dma((n,)), dma((n,)), dma((2 * n,)), dma((2 * n,)), dma((n,)), dma((n,)),
            dma((24,)), dma((24,)), dma((7,)), dma((7,)), dma((6,)), dma((6,)),
        ],
        compiler_params=pltpu.CompilerParams(
            collective_id=0, has_side_effects=True, vmem_limit_bytes=60 * 1024 * 1024
        ),
    )(
        session_length, event_owner[:, 0], event_row, price, price_dir, norm_gain,
        text_rows, image_rows, cotangent, w_query, w_key, w_value,
    )
    text_grad = gsum * image_rows.astype(jnp.float32)
    image_grad = gsum * text_rows.astype(jnp.float32)
    return (context, text_grad, image_grad)


def solution(mesh):
    fits = mesh.shape["dp"] == 16 and mesh.shape["mp"] == 2
    return jax.shard_map(
        local_16 if fits else local_any,
        mesh=mesh,
        in_specs=(
            P("dp"),
            P("dp", None),
            P("dp"),
            P("dp", "mp"),
            P("dp", "mp"),
            P("dp"),
            P("mp"),
            P("mp"),
            P("dp", "mp"),
            P("dp", "mp"),
            P("dp", "mp"),
            P("dp", "mp"),
        ),
        out_specs=(P("dp", "mp"), P("dp", "mp"), P("dp", "mp")),
        check_vma=False,
    )
```

```python
import math

import jax
import jax.numpy as jnp
from jax import lax
from jax.experimental import pallas as pl
from jax.experimental.pallas import tpu as pltpu
from jax.sharding import PartitionSpec as P

D = 4096
HD = 128
SLOT = 128


def fetch_rows(requests, text_rows, image_rows):
    row_ids = jnp.maximum(requests, 0)
    return (row_ids, text_rows[row_ids], image_rows[row_ids])


def join_rows(row_ids, text_got, image_got, price, price_dir):
    price_got = price[row_ids]
    mixed = text_got.astype(jnp.float32) * image_got.astype(jnp.float32) + price_got[
        ..., None
    ] * price_dir.astype(jnp.float32)
    return mixed.astype(jnp.bfloat16)


def answer(requests, text_rows, image_rows, price, price_dir):
    row_ids, text_got, image_got = fetch_rows(requests, text_rows, image_rows)
    joined_rows = join_rows(row_ids, text_got, image_got, price, price_dir)
    replies = lax.all_to_all(joined_rows, "dp", split_axis=0, concat_axis=0, tiled=True)
    return (replies, row_ids, text_got, image_got)


def credit_rows(row_ids, grad_rows, text_got, image_got, table_rows):
    col_width = grad_rows.shape[-1]
    flat_ids = row_ids.reshape(-1)
    grad_float = grad_rows.astype(jnp.float32)
    text_terms = (grad_float * image_got.astype(jnp.float32)).reshape(-1, col_width)
    image_terms = (grad_float * text_got.astype(jnp.float32)).reshape(-1, col_width)
    text_grad = jax.ops.segment_sum(text_terms, flat_ids, num_segments=table_rows)
    image_grad = jax.ops.segment_sum(image_terms, flat_ids, num_segments=table_rows)
    return (text_grad, image_grad)


def attend(query, keys, values, session_length):
    sessions = session_length.shape[0]
    heads_here = query.shape[1] // HD
    shape4 = (sessions, SLOT, heads_here, HD)
    scores = jnp.einsum(
        "sqhd,skhd->shqk",
        query.reshape(shape4),
        keys.reshape(shape4),
        preferred_element_type=jnp.float32,
    ) / math.sqrt(HD)
    position = jnp.arange(SLOT, dtype=jnp.int32)
    live_mask = position[None, :] < session_length[:, None]
    allowed = (position[None, :] <= position[:, None])[None, None, :, :] & live_mask[
        :, None, None, :
    ]
    scores = jnp.where(allowed, scores, jnp.float32(-1e30))
    row_max = jnp.max(scores, axis=-1, keepdims=True)
    powers = jnp.exp(scores - row_max)
    probs = (powers / jnp.sum(powers, axis=-1, keepdims=True)).astype(jnp.bfloat16)
    context = jnp.einsum(
        "shqk,skhd->sqhd", probs, values.reshape(shape4), preferred_element_type=jnp.float32
    )
    context = jnp.where(live_mask[:, :, None, None], context, jnp.float32(0.0))
    return context.reshape(sessions * SLOT, heads_here * HD).astype(jnp.bfloat16)


def local_any(
    session_length,
    event_owner,
    event_row,
    text_rows,
    image_rows,
    price,
    price_dir,
    norm_gain,
    w_query,
    w_key,
    w_value,
    cotangent,
):
    peers = lax.axis_size("dp")
    tok_count = event_row.shape[0]
    capacity = 2 * tok_count // peers
    col_width = text_rows.shape[1]
    table_rows = text_rows.shape[0]
    owner_ids = event_owner[:, 0]
    member = (owner_ids[:, None] == jnp.arange(peers, dtype=jnp.int32)[None, :]).astype(jnp.int32)
    earlier = jnp.sum((jnp.cumsum(member, axis=0) - member) * member, axis=1)
    slot_ids = owner_ids * capacity + earlier
    requests = (
        jnp.full((peers * capacity,), -1, jnp.int32)
        .at[slot_ids]
        .set(event_row)
        .reshape(peers, capacity)
    )
    grad_buffer = (
        jnp.zeros((peers * capacity, col_width), jnp.bfloat16)
        .at[slot_ids]
        .set(cotangent)
        .reshape(peers, capacity, col_width)
    )
    replies = answer(
        lax.all_to_all(requests, "dp", split_axis=0, concat_axis=0, tiled=True),
        text_rows,
        image_rows,
        price,
        price_dir,
    )[0]
    got_ids, got_grads = (
        lax.all_to_all(requests, "dp", split_axis=0, concat_axis=0, tiled=True),
        lax.all_to_all(grad_buffer, "dp", split_axis=0, concat_axis=0, tiled=True),
    )
    row_ids, text_got, image_got = fetch_rows(got_ids, text_rows, image_rows)
    text_grad, image_grad = credit_rows(row_ids, got_grads, text_got, image_got, table_rows)
    joined_rows = replies.reshape(peers * capacity, col_width)[slot_ids]
    joined_float = joined_rows.astype(jnp.float32)
    square_sums = lax.psum(jnp.sum(joined_float * joined_float, axis=1), "mp")
    scale = lax.rsqrt(square_sums / D + 1e-06)
    normed = (joined_float * scale[:, None] * norm_gain.astype(jnp.float32)[None, :]).astype(
        jnp.bfloat16
    )
    features_all = lax.all_gather(normed, "mp", axis=1, tiled=True)

    def add_rows(weight_rows):
        return jnp.dot(features_all, weight_rows, preferred_element_type=jnp.float32)

    query_sum = add_rows(lax.all_gather(w_query, "dp", axis=0, tiled=True))
    key_sum = add_rows(lax.all_gather(w_key, "dp", axis=0, tiled=True))
    value_sum = add_rows(lax.all_gather(w_value, "dp", axis=0, tiled=True))
    context = attend(
        query_sum.astype(jnp.bfloat16),
        key_sum.astype(jnp.bfloat16),
        value_sum.astype(jnp.bfloat16),
        session_length,
    )
    return (context, text_grad, image_grad)


def flip(index, bit):
    return index + bit - 2 * bit * ((index // bit) % 2)


def exchange_kernel(
    length_ref, owner_ref, row_ref, price_ref, dir_ref, gain_ref, text_hbm, image_hbm, cot_hbm,
    wq_ref, wk_ref, wv_ref,
    ctx_ref, gsum_ref,
    text_ref, image_ref, cot_ref, reqs_ref, probs_ref, ids, slots, tq, tsend, rep_out, rep_in, grad_out, grad_in,
    fvals, wbuf, xfull, xin, ss_out, ss_in, part_own, part_out, part_in,
    load_sem, id_s, id_r, rep_s, rep_r, grad_s, grad_r, w_s, w_r, one_s, one_r, p_s, p_r,
):
    me = lax.axis_index("dp")
    my_y = lax.axis_index("mp")
    n = 16
    cap = 16
    rel = me % 8
    half = me // 8
    far = flip(me, 8)
    wrows = wq_ref.shape[0]
    qw = wq_ref.shape[1]
    quarter = dir_ref.shape[0] // 2
    table = text_ref.shape[0]
    both_rows = 2 * SLOT
    weights_in = (wq_ref, wk_ref, wv_ref)
    table_loads = [
        pltpu.make_async_copy(a, b, load_sem.at[3 + k])
        for k, (a, b) in enumerate(
            ((text_hbm, text_ref), (image_hbm, image_ref), (cot_hbm, cot_ref))
        )
    ]
    w_loads = [
        pltpu.make_async_copy(w, wbuf.at[k, pl.ds(rel * wrows, wrows), :], load_sem.at[k])
        for k, w in enumerate(weights_in)
    ]
    for load in w_loads + table_loads:
        load.start()
    barrier = pltpu.get_barrier_semaphore()

    def greet(i, carry):
        pl.semaphore_signal(
            barrier, inc=1, device_id={"dp": (me + i) % n}, device_id_type=pl.DeviceIdType.MESH
        )
        return carry

    lax.fori_loop(1, n, greet, 0)
    pl.semaphore_signal(
        barrier, inc=1, device_id={"mp": 1 - my_y}, device_id_type=pl.DeviceIdType.MESH
    )
    pl.semaphore_signal(
        barrier, inc=1, device_id={"dp": far, "mp": 1 - my_y},
        device_id_type=pl.DeviceIdType.MESH,
    )

    def lanes(ref, rows):
        return jnp.broadcast_to(ref[...].reshape(1, ref.shape[0]), (rows, ref.shape[0]))

    owner_along = lanes(owner_ref, SLOT)
    before = lax.broadcasted_iota(jnp.int32, (SLOT, SLOT), 0) < lax.broadcasted_iota(
        jnp.int32, (SLOT, SLOT), 1
    )
    same = (jnp.transpose(owner_along) == owner_along) & before
    slot = owner_along[0:1, :] * cap + jnp.sum(same.astype(jnp.int32), axis=0, keepdims=True)
    picked = lax.broadcasted_iota(jnp.int32, (n * cap, SLOT), 0) == slot
    asked = jnp.max(jnp.where(picked, lanes(row_ref, n * cap), -1), axis=1, keepdims=True)
    reqs_ref[...] = jnp.broadcast_to(asked, (n * cap, 128))
    slots[half] = jnp.broadcast_to(slot, (8, SLOT))
    pl.semaphore_wait(barrier, n + 1)

    def remote(src, dst, send, recv, **to):
        return pltpu.make_async_remote_copy(
            src_ref=src, dst_ref=dst, send_sem=send, recv_sem=recv, device_id=to,
            device_id_type=pl.DeviceIdType.MESH,
        )

    def swap(src_of, dst, send, recv, base=0):
        def one(i):
            peer = (me + i) % n
            return remote(src_of(peer), dst, send.at[base + i], recv.at[base + i], dp=peer)

        def start(i, carry):
            one(i).start()
            return carry

        def finish(i, carry):
            one(i).wait_send()
            one(i).wait_recv()
            return carry

        return (
            lambda: lax.fori_loop(1, n, start, 0),
            lambda: lax.fori_loop(1, n, finish, 0),
        )

    def block(peer):
        return pl.ds(peer * cap, cap)

    id_start, id_finish = swap(
        lambda p: reqs_ref.at[block(p), :], ids.at[block(me), :], id_s, id_r
    )
    id_start()
    slot_out = remote(slots.at[half], slots.at[half], one_s.at[0], one_r.at[0], dp=far)
    slot_out.start()
    ids[block(me), :] = reqs_ref[block(me), :]

    def send_w(k, c, rel_index, bit, low=0, count=wrows):
        part = wbuf.at[k, pl.ds(rel_index * wrows + low, count), :]
        return remote(part, part, w_s.at[8 * k + c], w_r.at[8 * k + c], dp=flip(me, bit))

    zrows = wrows // 8
    own_x = [send_w(k, 0, rel, 2) for k in range(3)]
    own_z = [send_w(k, 1, rel, 4) for k in range(3)]
    own_c = [send_w(k, 2, rel, 1) for k in range(3)]
    x_on = [send_w(k, 3, flip(rel, 2), 4, 0, zrows) for k in range(3)]
    x_core = [send_w(k, 4, flip(rel, 2), 1) for k in range(3)]
    z_on = [send_w(k, 5, flip(rel, 4), 2, zrows, wrows - zrows) for k in range(3)]
    z_core = [send_w(k, 6, flip(rel, 4), 1) for k in range(3)]
    diag_core = [send_w(k, 7, flip(flip(rel, 2), 4), 1) for k in range(3)]

    def pass_on(k):
        own_x[k].wait_recv()
        x_on[k].start()
        x_core[k].start()
        own_z[k].wait_recv()
        z_on[k].start()
        z_core[k].start()

    def pass_diag(k):
        x_on[k].wait_recv()
        z_on[k].wait_recv()
        diag_core[k].start()

    w_loads[0].wait()
    own_x[0].start()
    own_z[0].start()
    own_c[0].start()
    for k in (1, 2):
        w_loads[k].wait()
        own_c[k].start()
    table_loads[0].wait()
    table_loads[1].wait()
    tile = 512
    tiles = quarter // tile
    price = jnp.transpose(lanes(price_ref, 128))[:, 0:1]
    dir_row = dir_ref[...].astype(jnp.float32).reshape(1, 2 * quarter)
    gain_row = gain_ref[...].astype(jnp.float32).reshape(1, 2 * quarter)
    fvals[0:1, :] = dir_row
    fvals[8:9, :] = gain_row

    def join(start, j):
        src = pl.ds(pl.multiple_of(start + j * tile, tile), tile)
        mixed = text_ref[:, src].astype(jnp.float32) * image_ref[:, src].astype(
            jnp.float32
        ) + price * fvals[0:1, src]
        gain = jnp.broadcast_to(fvals[8:9, src], (16, tile))
        return mixed.astype(jnp.bfloat16), gain.astype(jnp.bfloat16)

    def column(j):
        return pl.ds(pl.multiple_of(j * tile, tile), tile)

    def join_out(j, carry):
        rows, gain = join((1 - my_y) * quarter, j)
        tsend[0:table, column(j)] = rows
        tsend[table : table + 16, column(j)] = gain
        return carry

    def join_own(j, carry):
        rows, gain = join(my_y * quarter, j)
        tq[my_y, 0:table, column(j)] = rows
        tq[my_y, table : table + 16, column(j)] = gain
        return carry

    def piece(c):
        return pl.ds(c * tile, tile)

    table_out = [
        remote(
            tsend.at[:, piece(c)], tq.at[my_y, :, piece(c)], one_s.at[5 + c], one_r.at[5 + c],
            mp=1 - my_y,
        )
        for c in range(tiles)
    ]
    for c in range(tiles):
        join_out(c, 0)
        table_out[c].start()
    lax.fori_loop(0, tiles, join_own, 0)

    def pick_of(slot):
        return (
            lax.broadcasted_iota(jnp.int32, (n * cap, SLOT), 0) == slot
        ).astype(jnp.float32).astype(jnp.bfloat16)

    id_finish()
    got = ids[...]
    lane = lax.broadcasted_iota(jnp.int32, got.shape, 1)
    want = jnp.concatenate(
        [(got == lane + 128 * k).astype(jnp.float32) for k in range(table // 128)], axis=1
    ).astype(jnp.bfloat16)
    replies = [
        swap(
            lambda p, c=c: rep_out.at[p // 8, :, block(p % 8), piece(c)],
            rep_in.at[:, block(me), piece(c)],
            rep_s, rep_r, c * n,
        )
        for c in range(tiles)
    ]
    for c in range(tiles):
        table_out[c].wait_send()
        table_out[c].wait_recv()
        for m in range(2):
            rows = jnp.dot(
                want, tq[m, 0:table, piece(c)], preferred_element_type=jnp.float32
            ).astype(jnp.bfloat16)
            rep_out[m, 0, :, piece(c)] = rows[: 8 * cap]
            rep_out[m, 1, :, piece(c)] = rows[8 * cap :]
        replies[c][0]()
    own_x[1].start()
    rep_in[:, block(me), :] = rep_out[half, :, block(rel), :]
    table_loads[2].wait()
    pick = pick_of(slots[half, 0:1, :])

    def pack_grads(j, carry):
        grad_out[:, column(j)] = jnp.dot(
            pick, cot_ref[:, column(j)], preferred_element_type=jnp.float32
        ).astype(jnp.bfloat16)
        return carry

    lax.fori_loop(0, 2 * tiles, pack_grads, 0)
    pass_on(0)
    slot_out.wait_send()
    slot_out.wait_recv()
    chosen = [pick_of(slots[zs, 0:1, :]) for zs in range(2)]
    across = []
    for c in range(tiles):
        replies[c][1]()
        if c == tiles - 1:
            own_z[1].start()
            own_x[2].start()
        for zs in range(2):
            xfull[my_y, zs * SLOT : (zs + 1) * SLOT, piece(c)] = lax.dot_general(
                chosen[zs], rep_in[zs, :, piece(c)], (((0,), (0,)), ((), ())),
                preferred_element_type=jnp.float32,
            ).astype(jnp.bfloat16)
        xfull[my_y, both_rows : both_rows + 16, piece(c)] = tq[
            half, table : table + 16, piece(c)
        ]
        part = xfull.at[my_y, :, piece(c)]
        across.append(remote(part, part, one_s.at[1 + c], one_r.at[1 + c], mp=1 - my_y))
        across[c].start()
    grad_start, grad_finish = swap(
        lambda p: grad_out.at[block(p), :], grad_in.at[block(me), :], grad_s, grad_r
    )
    own_z[2].start()

    def squares(q):
        def add(j, total):
            a = xfull[q, 0:both_rows, column(j)].astype(jnp.float32)
            return total + jnp.sum(a * a, axis=1, keepdims=True)

        return lax.fori_loop(0, tiles, add, jnp.zeros((both_rows, 1), jnp.float32))

    near = squares(my_y)
    ss_out[...] = jnp.transpose(jnp.broadcast_to(near, (both_rows, 128)))[0:8, :]
    ss_far = remote(ss_out, ss_in.at[0], one_s.at[3], one_r.at[3], dp=far)
    ss_far.start()
    ss_diag = remote(ss_out, ss_in.at[1], one_s.at[4], one_r.at[4], dp=far, mp=1 - my_y)
    ss_diag.start()
    pass_diag(0)
    for copy in across:
        copy.wait_send()
        copy.wait_recv()
    near = near + squares(1 - my_y)
    for copy in (ss_far, ss_diag):
        copy.wait_send()
        copy.wait_recv()
    beyond = ss_in[0] + ss_in[1]
    beyond = jnp.transpose(jnp.broadcast_to(beyond[0:1, :], (128, both_rows)))[:, 0:1]
    scale = lax.rsqrt((near + beyond) / D + 1e-06)
    for q in range(2):

        def norm(j, carry, q=q):
            normed = (
                xfull[q, 0:both_rows, column(j)].astype(jnp.float32)
                * scale
                * xfull[q, both_rows : both_rows + 1, column(j)].astype(jnp.float32)
            )
            xin[:, column(q * tiles + j)] = normed.astype(jnp.bfloat16)
            return carry

        lax.fori_loop(0, tiles, norm, 0)

    wide = 256
    sends = []
    for k in range(3):
        if k:
            pass_on(k)
            if k == 1:
                grad_start()
                grad_in[block(me), :] = grad_out[block(me), :]
            pass_diag(k)
        own_c[k].wait_recv()
        x_core[k].wait_recv()
        z_core[k].wait_recv()
        diag_core[k].wait_recv()

        def project(j, carry, k=k):
            at = pl.ds(pl.multiple_of(j * wide, wide), wide)
            both = jnp.dot(xin[...], wbuf[k, :, at], preferred_element_type=jnp.float32)
            for zs in range(2):
                rows = both[zs * SLOT : (zs + 1) * SLOT]
                part_own[k, zs, :, at] = rows
                part_out[k, zs, :, at] = rows.astype(jnp.bfloat16)
            return carry

        steps = qw // wide // 2
        for h in range(2):
            lax.fori_loop(h * steps, (h + 1) * steps, project, 0)
            cols = pl.ds(h * (qw // 2), qw // 2)
            send = remote(
                part_out.at[k, 1 - half, :, cols], part_in.at[k, :, cols],
                p_s.at[2 * k + h], p_r.at[2 * k + h], dp=far,
            )
            send.start()
            sends.append(send)

    key_at = lax.broadcasted_iota(jnp.int32, (SLOT, SLOT), 1)
    query_at = lax.broadcasted_iota(jnp.int32, (SLOT, SLOT), 0)
    length = length_ref[0]
    allowed = (key_at <= query_at) & (key_at < length)
    live = query_at < length

    def whole(k, at):
        total = part_own[k, half, :, at] + part_in[k, :, at].astype(jnp.float32)
        return total.astype(jnp.bfloat16)

    def head_columns(h):
        return pl.ds(pl.multiple_of(h * HD, HD), HD)

    def head_probs(h, carry):
        at = head_columns(h)
        scores = lax.dot_general(
            whole(0, at), whole(1, at), (((1,), (1,)), ((), ())),
            preferred_element_type=jnp.float32,
        ) / math.sqrt(HD)
        scores = jnp.where(allowed, scores, jnp.float32(-1e30))
        powers = jnp.exp(scores - jnp.max(scores, axis=-1, keepdims=True))
        probs_ref[h] = (powers / jnp.sum(powers, axis=-1, keepdims=True)).astype(jnp.bfloat16)
        return carry

    def head_context(h, carry):
        at = head_columns(h)
        context = jnp.dot(probs_ref[h], whole(2, at), preferred_element_type=jnp.float32)
        ctx_ref[:, at] = jnp.where(live, context, jnp.float32(0.0)).astype(jnp.bfloat16)
        return carry

    for send in sends[:4]:
        send.wait_recv()
    lax.fori_loop(0, qw // HD, head_probs, 0)
    grad_finish()

    def credit(j, carry):
        gsum_ref[:, column(j)] = lax.dot_general(
            want, grad_in[:, column(j)], (((0,), (0,)), ((), ())),
            preferred_element_type=jnp.float32,
        )
        return carry

    lax.fori_loop(0, 2 * tiles, credit, 0)
    for group in (own_x, own_z, own_c, x_on, x_core, z_on, z_core, diag_core):
        for copy in group:
            copy.wait_send()
    half_heads = qw // HD // 2
    for h in range(2):
        sends[4 + h].wait_recv()
        lax.fori_loop(h * half_heads, (h + 1) * half_heads, head_context, 0)
    for send in sends:
        send.wait_send()


def local_16(
    session_length, event_owner, event_row, text_rows, image_rows, price, price_dir, norm_gain,
    w_query, w_key, w_value, cotangent,
):
    n = 16
    cap = 16
    tokens = event_row.shape[0]
    width = text_rows.shape[1]
    table = text_rows.shape[0]
    wrows, qw = w_query.shape
    vmem = pl.BlockSpec(memory_space=pltpu.VMEM)
    hbm = pl.BlockSpec(memory_space=pl.ANY)
    dma = pltpu.SemaphoreType.DMA
    bf16 = jnp.bfloat16
    context, gsum = pl.pallas_call(
        exchange_kernel,
        out_shape=(
            jax.ShapeDtypeStruct((tokens, qw), bf16),
            jax.ShapeDtypeStruct((table, width), jnp.float32),
        ),
        in_specs=[pl.BlockSpec(memory_space=pltpu.SMEM)] + [vmem] * 5 + [hbm] * 6,
        out_specs=(vmem, vmem),
        scratch_shapes=[
            pltpu.VMEM((table, width), bf16),
            pltpu.VMEM((table, width), bf16),
            pltpu.VMEM((tokens, width), bf16),
            pltpu.VMEM((n * cap, 128), jnp.int32),
            pltpu.VMEM((qw // HD, tokens, tokens), bf16),
            pltpu.VMEM((n * cap, 128), jnp.int32),
            pltpu.VMEM((2, 8, tokens), jnp.int32),
            pltpu.VMEM((2, table + 16, width // 2), bf16),
            pltpu.VMEM((table + 16, width // 2), bf16),
            pltpu.VMEM((2, 2, 8 * cap, width // 2), bf16),
            pltpu.VMEM((2, n * cap, width // 2), bf16),
            pltpu.VMEM((n * cap, width), bf16),
            pltpu.VMEM((n * cap, width), bf16),
            pltpu.VMEM((16, width), jnp.float32),
            pltpu.VMEM((3, 8 * wrows, qw), bf16),
            pltpu.VMEM((2, 2 * tokens + 16, width // 2), bf16),
            pltpu.VMEM((2 * tokens, width), bf16),
            pltpu.VMEM((8, 2 * tokens), jnp.float32),
            pltpu.VMEM((2, 8, 2 * tokens), jnp.float32),
            pltpu.VMEM((3, 2, tokens, qw), jnp.float32),
            pltpu.VMEM((3, 2, tokens, qw), bf16),
            pltpu.VMEM((3, tokens, qw), bf16),
            dma((6,)), dma((n,)), dma((n,)), dma((2 * n,)), dma((2 * n,)), dma((n,)), dma((n,)),
            dma((24,)), dma((24,)), dma((7,)), dma((7,)), dma((6,)), dma((6,)),
        ],
        compiler_params=pltpu.CompilerParams(
            collective_id=0, has_side_effects=True, vmem_limit_bytes=60 * 1024 * 1024
        ),
    )(
        session_length, event_owner[:, 0], event_row, price, price_dir, norm_gain,
        text_rows, image_rows, cotangent, w_query, w_key, w_value,
    )
    text_grad = gsum * image_rows.astype(jnp.float32)
    image_grad = gsum * text_rows.astype(jnp.float32)
    return (context, text_grad, image_grad)


def solution(mesh):
    fits = mesh.shape["dp"] == 16 and mesh.shape["mp"] == 2
    return jax.shard_map(
        local_16 if fits else local_any,
        mesh=mesh,
        in_specs=(
            P("dp"),
            P("dp", None),
            P("dp"),
            P("dp", "mp"),
            P("dp", "mp"),
            P("dp"),
            P("mp"),
            P("mp"),
            P("dp", "mp"),
            P("dp", "mp"),
            P("dp", "mp"),
            P("dp", "mp"),
        ),
        out_specs=(P("dp", "mp"), P("dp", "mp"), P("dp", "mp")),
        check_vma=False,
    )
```
